256 devices in a mesh: tm: 64 (over z, y_hi, x), patch: 4 (over y_lo, core).
Axes of the slice: x: 4, y: 4 (y_hi: 2, y_lo: 2; y = y_hi * 2 + y_lo), z: 8, core: 2. Of those that a mesh axis runs over, the one named last changes fastest.
Arguments:
- tokens: float32 [1, 128, 256, 768], P(None, 'tm', 'patch'), may hold values from -6 to 6
- norm_gain_vector: float32 [768], replicated, may hold values from 0.1 to 1.9
- qkv_weight: float32 [768, 2304], replicated, may hold values from -4 to 4
- out_weight: float32 [768, 768], replicated, may hold values from -0.21875 to 0.21875
- upstream: float32 [1, 128, 256, 768], P(None, 'tm', 'patch'), may hold values from -6 to 6
Outputs:
- output: float32 [1, 128, 256, 768], P(None, 'tm', 'patch')
- tokens_grad: float32 [1, 128, 256, 768], P(None, 'tm', 'patch')
- qkv_grad: float32 [768, 2304], P('tm')
- out_grad: float32 [768, 768], P('tm')
- gain_grad: float32 [768], P('tm')
The draws below stay inside these ranges and needn't reach their ends.
All inputs are finite; a program needn't handle non-finite values.
Results may differ from the reference program's by a relative error of at most 0.0003.
Values sent between devices are 32-bit elements; how exact they have to be, the bound alone decides.
A program may use at most 128 MiB of HBM per device.

```python
import math
import jax
import jax.numpy as jnp
from jax import lax

D = 768
HEADS = 12
HEAD_DIM = 64
CLIPS = 1
FRAMES = 128
PATCHES = 256


def draw_tokens(key, part):
    key = jax.random.fold_in(key, 11)
    shape = (CLIPS, FRAMES, PATCHES, D)
    result = jax.random.normal(key, shape, jnp.float32)
    return jnp.clip(result, -6.0, 6.0).astype(jnp.float32)


def draw_qkv_weight(key, part):
    key = jax.random.fold_in(key, 12)
    second_result = jax.random.fold_in(key, 1)
    scale = 1.0 / math.sqrt(D)
    result = jax.random.normal(second_result, (D, 3 * D), jnp.float32) * scale
    return jnp.clip(result, -4.0, 4.0).astype(jnp.float32)


def block_scale(own_key, shape, cuts, low, top_value):
    loudness = 1.0
    for dim, parts in cuts:
        draws = jax.random.uniform(jax.random.fold_in(jax.random.fold_in(own_key, 6), dim), (parts,), jnp.float32, low / len(cuts), top_value / len(cuts))
        loudness = loudness * jnp.repeat(jnp.exp(draws), shape[dim] // parts).reshape((-1,) + (1,) * (len(shape) - 1 - dim))
    return loudness


def noise(key, dims, deviation, bound, cuts=(), held_as=jnp.bfloat16):
    factor_of = block_scale(key, dims, cuts, -0.22, 0.18) if cuts else 1.0
    drawn = jax.random.normal(key, dims, jnp.float32) * deviation * factor_of
    return jnp.minimum(jnp.maximum(drawn, -bound), bound).astype(held_as)


def setup_inputs(seed: int = 0) -> dict:
    arg_keys = jax.random.split(jax.random.key(seed), 6)
    return {
        "tokens": draw_tokens(jax.random.fold_in(arg_keys[5], 71), 0),
        "norm_gain_vector": jnp.clip(1.0 + 0.18 * jax.random.normal(arg_keys[1], (D,), jnp.float32), 0.1, 1.9),
        "qkv_weight": draw_qkv_weight(jax.random.fold_in(arg_keys[5], 71), 0),
        "out_weight": noise(arg_keys[3], (D, D), D ** -0.5, 0.21875, (), jnp.float32),
        "upstream": noise(arg_keys[4], (CLIPS, FRAMES, PATCHES, D), 1.0, 6.0, ((1, 64), (2, 4)), jnp.float32),
    }


HIGH = lax.Precision.HIGHEST

def sublayer(tokens, norm_gain_vector, qkv_weight, out_weight):
    input_average = lax.optimization_barrier(jnp.mean(tokens, axis=-1, keepdims=True))
    centered_input = tokens - input_average
    var = lax.optimization_barrier(jnp.mean(centered_input * centered_input, axis=-1, keepdims=True))
    normalized_input = centered_input * lax.rsqrt(var + 1e-05) * norm_gain_vector
    qkv = jnp.einsum('bfpd,de->bfpe', normalized_input, qkv_weight, precision=HIGH)
    shape = qkv.shape[:3] + (3, HEADS, HEAD_DIM)
    qkv = qkv.reshape(shape)
    query, keys, values = (qkv[:, :, :, 0], qkv[:, :, :, 1], qkv[:, :, :, 2])
    scores = jnp.einsum('bfphe,bgphe->bphfg', query, keys, precision=HIGH) / jnp.sqrt(jnp.float32(HEAD_DIM))
    probs = jax.nn.softmax(scores, axis=-1)
    mix = jnp.einsum('bphfg,bgphe->bfphe', probs, values, precision=HIGH)
    mix = mix.reshape(tokens.shape)
    return tokens + jnp.einsum('bfpd,de->bfpe', mix, out_weight, precision=HIGH)

def reference(tokens, norm_gain_vector, qkv_weight, out_weight, upstream):
    output, pullback = jax.vjp(sublayer, tokens, norm_gain_vector, qkv_weight, out_weight)
    tokens_grad, gain_grad, qkv_grad, out_grad = pullback(upstream)
    return (output, tokens_grad, qkv_grad, out_grad, gain_grad)
```

```python
import functools

import jax
import jax.numpy as jnp
from jax import lax
from jax.experimental import pallas as pl
from jax.experimental.pallas import tpu as pltpu
from jax.sharding import PartitionSpec as P

F32, BF16 = jnp.float32, jnp.bfloat16
MESH = pl.DeviceIdType.MESH


def split(a):
    hi = a.astype(BF16)
    return hi, (a - hi.astype(F32)).astype(BF16)

def dot(a, b, ca=1, cb=0):
    return lax.dot_general(a, b, (((ca,), (cb,)), ((), ())), preferred_element_type=F32)

def rows2(a, b): return jnp.concatenate([a, b], 0)
def cols2(a, b): return jnp.concatenate([a, b], 1)

def product(a_hi, a_lo, b_hi, b_lo, cb=0):
    m = a_hi.shape[0]
    both = dot(rows2(a_hi, a_lo), b_hi, 1, cb)
    return both[:m] + both[m:] + dot(a_hi, b_lo, 1, cb)

def head_pair(x):
    lane = lax.broadcasted_iota(jnp.int32, x.shape, 1)
    first = lane < 64
    return split(rows2(jnp.where(first, x, 0.0), jnp.where(first, 0.0, x)))

def by_heads(x, pair):
    hi, lo = split(x)
    p_hi, p_lo = pair
    return dot(cols2(hi, lo), cols2(p_hi, p_hi), 1, 1) + dot(hi, p_lo, 1, 1)

def mix_heads(x, pair):
    hi, lo = split(x)
    p_hi, p_lo = pair
    both = dot(hi, cols2(p_hi, p_lo))
    return both[:, :128] + both[:, 128:] + dot(lo, p_hi)

def back_heads(x, y):
    hi, lo = split(x.T)
    y_hi, y_lo = split(y)
    both = dot(hi, cols2(y_hi, y_lo))
    r = both[:, :128] + both[:, 128:] + dot(lo, y_hi)
    lane = lax.broadcasted_iota(jnp.int32, (128, 128), 1)
    return jnp.where(lane < 64, r[:128], r[128:])

def prep_weights(w, wh, wl, step):
    for n in range(0, w.shape[1], step):
        hi, lo = split(w[:, n:n + step])
        wh[:, n:n + step] = hi
        wl[:, n:n + step] = lo

def forward(t, gain, wqh, wql, woh, wol, xhat_ref, inv_ref, qkv, probs, mix, out):
    mean = jnp.mean(t, axis=1, keepdims=True)
    cen = t - mean
    inv = lax.rsqrt(jnp.mean(cen * cen, axis=1, keepdims=True) + 1e-5)
    xhat = cen * inv
    xhat_ref[...] = xhat
    inv_ref[...] = jnp.broadcast_to(inv, inv_ref.shape)
    n_hi, n_lo = split(xhat * gain)
    for n in range(0, 2304, 256):
        r = product(n_hi, n_lo, wqh[:, n:n + 256], wql[:, n:n + 256])
        qkv[:, n:n + 256] = r * 0.125 if n < 768 else r
    for p in range(6):
        c = 128 * p
        s = by_heads(qkv[:, c:c + 128], head_pair(qkv[:, 768 + c:768 + c + 128]))
        ps = []
        for h in range(2):
            e = s[:, 128 * h:128 * h + 128]
            e = jnp.exp(e - jnp.max(e, axis=1, keepdims=True))
            ps.append(e / jnp.sum(e, axis=1, keepdims=True))
        pr = cols2(*ps)
        probs[:, 256 * p:256 * p + 256] = pr
        mix[:, c:c + 128] = mix_heads(pr, head_pair(qkv[:, 1536 + c:1536 + c + 128]))
    m_hi, m_lo = split(mix[...])
    for n in range(0, 768, 256):
        out[:, n:n + 256] = t[:, n:n + 256] + product(m_hi, m_lo, woh[:, n:n + 256], wol[:, n:n + 256])

def backward_attn(u, woh, wol, qkv, probs, dmix, dqkv):
    u_hi, u_lo = split(u)
    for n in range(0, 768, 256):
        dmix[:, n:n + 256] = product(u_hi, u_lo, woh[n:n + 256, :], wol[n:n + 256, :], 1)
    for p in range(6):
        c = 128 * p
        do = dmix[:, c:c + 128]
        pr = probs[:, 256 * p:256 * p + 256]
        dqkv[:, 1536 + c:1536 + c + 128] = back_heads(pr, do)
        dp = by_heads(do, head_pair(qkv[:, 1536 + c:1536 + c + 128]))
        ds = []
        for h in range(2):
            a, b = pr[:, 128 * h:128 * h + 128], dp[:, 128 * h:128 * h + 128]
            ds.append(a * (b - jnp.sum(a * b, axis=1, keepdims=True)))
        ds = cols2(*ds)
        dqkv[:, c:c + 128] = 0.125 * mix_heads(ds, head_pair(qkv[:, 768 + c:768 + c + 128]))
        dqkv[:, 768 + c:768 + c + 128] = back_heads(ds, qkv[:, c:c + 128])

def backward_norm(u, gain, wqh, wql, xhat_ref, inv_ref, dqkv, tg):
    d_hi, d_lo = split(dqkv[...])
    for n in range(0, 768, 256):
        tg[:, n:n + 256] = product(d_hi, d_lo, wqh[n:n + 256, :], wql[n:n + 256, :], 1)
    dn = tg[...] * gain
    xhat = xhat_ref[...]
    first = jnp.mean(dn, axis=1, keepdims=True)
    second = jnp.mean(dn * xhat, axis=1, keepdims=True)
    tg[...] = u + inv_ref[:, :1] * (dn - first - xhat * second)

def weight_product(left_t, right, store):
    l_hi, l_lo = left_t
    r_hi, r_lo = right
    lhs = jnp.concatenate([l_hi, l_lo, l_hi], 1)
    rhs = jnp.concatenate([r_hi, r_hi, r_lo], 0)
    store(dot(lhs, rhs))


def place():
    return lax.axis_index("tm"), lax.axis_index("patch")


def pack(value, send):
    for i in range(2):
        for c in range(6):
            send[:, 6 * i + c, :] = value[64 * i:64 * i + 64, 128 * c:128 * c + 128]


def unpack(received, store):
    for i in range(2):
        for c in range(6):
            store(i, c, received[:, 6 * i + c, :])


def greet(extra):
    t, q = place()
    barrier = pltpu.get_barrier_semaphore()

    @pl.loop(1, 64)
    def _(k):
        pl.semaphore_signal(barrier, inc=1, device_id=(t ^ k, q), device_id_type=MESH)

    for peer in extra:
        pl.semaphore_signal(barrier, inc=1, device_id=peer, device_id_type=MESH)
    pl.semaphore_wait(barrier, 63 + len(extra))


def exchange_start(send, received, sems):
    t, q = place()

    @pl.loop(1, 64)
    def _(k):
        peer = lax.rem(t + k, 64)
        pltpu.make_async_remote_copy(
            send.at[peer], received.at[t], sems.at[0], sems.at[1], device_id=(peer, q), device_id_type=MESH
        ).start()

    received[pl.ds(t, 1)] = send[pl.ds(t, 1)]


def exchange_wait(send, received, sems):
    t, q = place()
    all_bytes = pltpu.make_async_remote_copy(
        send.at[pl.ds(0, 63)], received.at[pl.ds(0, 63)], sems.at[0], sems.at[1], device_id=(t ^ 1, q), device_id_type=MESH
    )
    all_bytes.wait_send()
    all_bytes.wait_recv()


def arrive_kernel(tok, up, t_out, u_out, send_t, send_u, recv_t, recv_u, sem_t, sem_u):
    pack(tok, send_t)
    pack(up, send_u)
    greet([])
    exchange_start(send_t, recv_t, sem_t)
    exchange_start(send_u, recv_u, sem_u)
    for recv, send, sem, o in ((recv_t, send_t, sem_t, t_out), (recv_u, send_u, sem_u, u_out)):
        exchange_wait(send, recv, sem)

        def store(i, c, v, o=o):
            o[64 * i:64 * i + 64, 128 * c:128 * c + 128] = v

        unpack(recv, store)


def layer_kernel(t_ref, u_ref, g_ref, wq_ref, wo_ref, out, tg, xhat, mix, dqkv, wrows, wqh, wql, woh, wol, inv, qkv, probs, dmix):
    prep_weights(wq_ref, wqh, wql, 256)
    prep_weights(wo_ref, woh, wol, 256)
    own_rows(wq_ref, wrows)
    forward(t_ref[...], g_ref[...], wqh, wql, woh, wol, xhat, inv, qkv, probs, mix, out)
    backward_attn(u_ref[...], woh, wol, qkv, probs, dmix, dqkv)
    backward_norm(u_ref[...], g_ref[...], wqh, wql, xhat, inv, dqkv, tg)


def own_rows(w_ref, rows):
    t, _ = place()
    base = pl.multiple_of(t // 2 * 24 + lax.rem(t, 2) * 8, 8)
    wide = w_ref[pl.ds(base, 16), :]
    rows[...] = jnp.where(lax.rem(t, 2) == 0, wide[:12], wide[4:])


def bits():
    t, q = place()
    x, yh, yl = lax.rem(t, 4), lax.rem(t // 4, 2), q // 2
    return {"a": lax.rem(x, 2) ^ (x // 2), "b": x // 2, "c": yl ^ yh, "d": yh}


def partner(dim):
    t, q = place()
    return {"a": (t ^ 1, q), "b": (t ^ 3, q), "c": (t, q ^ 2), "d": (t ^ 4, q ^ 2)}[dim]


DIMS = "abcd"
AXIS = {"a": 0, "c": 1, "d": 3, "b": 4}


def order(part):
    return [DIMS[(part + s) % 4] for s in range(4)]


def extents(part, step):
    size = [2, 2, 2, 2, 2]
    for dim in order(part)[:step + 1]:
        size[AXIS[dim]] = 1
    return size


def select(part, step, own, other):
    at = [pl.ds(0, 2), pl.ds(0, 2), pl.ds(2 * part, 2), pl.ds(0, 2), pl.ds(0, 2)]
    for s, dim in enumerate(order(part)[:step + 1]):
        bit = own[dim]
        at[AXIS[dim]] = pl.ds(1 - bit if other and s == step else bit, 1)
    return tuple(at)


def reduce_start(part, step, own, terms, landing, sems):
    copy = pltpu.make_async_remote_copy(
        terms.at[select(part, step, own, True)],
        landing[step][part],
        sems.at[0, step, part],
        sems.at[1, step, part],
        device_id=partner(order(part)[step]),
        device_id_type=MESH,
    )
    copy.start()
    return copy


def reduce_add(part, step, own, terms, landing):
    at = select(part, step, own, False)
    size = extents(part, step)
    buf = landing[step][part]
    for i in range(size[0]):
        for j in range(size[1]):
            for k in range(size[2]):
                for m in range(size[3]):
                    for n in range(size[4]):
                        idx = tuple(s.start + o for s, o in zip(at, (i, j, k, m, n)))
                        terms[idx] = terms[idx] + buf[i, j, k, m, n]


def landing_shapes():
    return [pltpu.VMEM(tuple(extents(part, step)) + (24, 384), F32) for step in range(4) for part in range(4)]


def group_peers():
    t, q = place()
    return [(t ^ dx, q ^ dq) for dx in (0, 1) for dq in range(4) if dx or dq]


def sibling_start(pairs, sems):
    t, q = place()
    copies = []
    for k, (src, dst) in enumerate(pairs):
        copy = pltpu.make_async_remote_copy(src, dst, sems.at[0, k], sems.at[1, k], device_id=(t, q ^ 1), device_id_type=MESH)
        copy.start()
        copies.append(copy)
    return copies


def return_kernel(
    out_in, tg_in, xhat, mix, dqkv, u, g_ref, wrows,
    out, tg, qkv_rows, out_rows, gain_rows,
    send_o, send_g, recv_o, recv_g, terms, s_xhat, s_mix, s_dqkv, s_up, recv_z, own_piece, pieces,
    *rest,
):
    landing = [rest[4 * s:4 * s + 4] for s in range(4)]
    sem_o, sem_g, sem_sib, sem_red, sem_z, sem_p = rest[16:]
    t, q = place()
    core = lax.rem(q, 2)
    own = bits()
    peers = group_peers()
    greet([p for k, p in enumerate(peers) if k != 3] + [(t ^ 4, q ^ 2)])
    theirs, mine = (1 - core) * 1152, core * 1152
    sib = sibling_start(
        [
            (xhat, s_xhat),
            (dqkv.at[:, pl.ds(pl.multiple_of(theirs, 128), 1152)], s_dqkv),
            (mix, s_mix),
            (u.at[:, pl.ds(pl.multiple_of((1 - core) * 384, 128), 384)], s_up),
        ],
        sem_sib,
    )
    pack(out_in, send_o)
    exchange_start(send_o, recv_o, sem_o)
    pack(tg_in, send_g)
    exchange_start(send_g, recv_g, sem_g)
    for copy in sib:
        copy.wait()
    left = split(rows2(xhat[...], s_xhat[...]).T)
    for j in range(4):
        if j < 3:
            col = pl.ds(pl.multiple_of(mine + 384 * j, 128), 384)
            right = split(rows2(dqkv[:, col], s_dqkv[:, 384 * j:384 * j + 384]))
        else:
            left = split(rows2(mix[...], s_mix[...]).T)
            col = pl.ds(pl.multiple_of(core * 384, 128), 384)
            right = split(rows2(u[:, col], s_up[...]))

        def store(v, j=j):
            terms[j // 2, j % 2] = v.reshape(8, 2, 2, 24, 384)

        weight_product(left, right, store)
    for step in range(4):
        copies = [reduce_start(p, step, own, terms, landing, sem_red) for p in range(4)]
        for p in range(4):
            copies[p].wait()
            reduce_add(p, step, own, terms, landing)
    z = t // 8
    held = terms.at[own["a"], own["c"], :, own["d"], own["b"]]

    @pl.loop(1, 8)
    def _(k):
        pz = z ^ k
        pltpu.make_async_remote_copy(
            held.at[pz], recv_z.at[z], sem_z.at[0], sem_z.at[1], device_id=(t ^ (8 * k), q), device_id_type=MESH
        ).start()

    recv_z[pl.ds(z, 1)] = held[pl.ds(z, 1)]
    every = pltpu.make_async_remote_copy(
        recv_z.at[pl.ds(0, 7)], recv_z.at[pl.ds(0, 7)], sem_z.at[0], sem_z.at[1], device_id=(t ^ 8, q), device_id_type=MESH
    )
    every.wait_send()
    every.wait_recv()
    total = recv_z[0]
    for k in range(1, 8):
        total = total + recv_z[k]
    own_piece[0] = total[:12]
    own_piece[1] = total[12:]
    me = core * 4 + own["a"] * 2 + own["c"]
    copies = []
    for k, (pt, pq) in enumerate(peers):
        copy = pltpu.make_async_remote_copy(
            own_piece.at[lax.rem(pt, 2)], pieces.at[me], sem_p.at[0, k], sem_p.at[1, k], device_id=(pt, pq), device_id_type=MESH
        )
        copy.start()
        copies.append(copy)
    pieces[pl.ds(me, 1)] = own_piece[pl.ds(lax.rem(t, 2), 1)]
    for copy in copies:
        copy.wait()
    lane = lax.broadcasted_iota(jnp.int32, (12, 768), 1)
    row = lax.broadcasted_iota(jnp.int32, (12, 768), 0)
    gain = jnp.sum(jnp.where(lane == row + 12 * t, g_ref[...], 0.0), axis=1, keepdims=True)
    gain_sum = jnp.zeros((12, 1), F32)
    for k in range(8):
        j, c = k % 4, k // 4
        piece = pieces[k]
        if j < 3:
            col = 1152 * c + 384 * j
            qkv_rows[:, col:col + 384] = piece * gain
            gain_sum = gain_sum + jnp.sum(piece * wrows[:, col:col + 384], axis=1, keepdims=True)
        else:
            out_rows[:, 384 * c:384 * c + 384] = piece
    gain_rows[...] = jnp.broadcast_to(gain_sum, (12, 128))
    for send, recv, sem, o in ((send_o, recv_o, sem_o, out), (send_g, recv_g, sem_g, tg)):
        exchange_wait(send, recv, sem)

        def store(i, c, v, o=o):
            o[64 * i:64 * i + 64, 128 * c:128 * c + 128] = v

        unpack(recv, store)


def body(tokens, norm_gain_vector, qkv_weight, out_weight, upstream):
    shape = tokens.shape
    tok, up = tokens.reshape(128, 768), upstream.reshape(128, 768)
    gain = norm_gain_vector.reshape(1, 768)
    vmem = pl.BlockSpec(memory_space=pltpu.VMEM)
    S = lambda *s: jax.ShapeDtypeStruct(s, F32)
    V = lambda *s: pltpu.VMEM(s, F32)
    H = lambda *s: pltpu.VMEM(s, BF16)
    D = lambda *s: pltpu.SemaphoreType.DMA(s)
    big = 56 * 2 ** 20
    t_in, u_in = pl.pallas_call(
        arrive_kernel,
        out_shape=[S(128, 768)] * 2,
        in_specs=[vmem] * 2,
        out_specs=[vmem] * 2,
        scratch_shapes=[V(64, 12, 128)] * 4 + [D(2), D(2)],
        compiler_params=pltpu.CompilerParams(collective_id=0, has_side_effects=True, vmem_limit_bytes=big),
    )(tok, up)
    out_in, tg_in, xhat, mix, dqkv, wrows = pl.pallas_call(
        layer_kernel,
        out_shape=[S(128, 768), S(128, 768), S(128, 768), S(128, 768), S(128, 2304), S(12, 2304)],
        in_specs=[vmem] * 5,
        out_specs=[vmem] * 6,
        scratch_shapes=[
            H(768, 2304), H(768, 2304), H(768, 768), H(768, 768),
            V(128, 128), V(128, 2304), V(128, 1536), V(128, 768),
        ],
        compiler_params=pltpu.CompilerParams(vmem_limit_bytes=big),
    )(t_in, u_in, gain, qkv_weight, out_weight)
    out, tg, qkv_rows, out_rows, gain_rows = pl.pallas_call(
        return_kernel,
        out_shape=[S(128, 768), S(128, 768), S(12, 2304), S(12, 768), S(12, 128)],
        in_specs=[vmem] * 8,
        out_specs=[vmem] * 5,
        scratch_shapes=[V(64, 12, 128)] * 4
        + [V(2, 2, 8, 2, 2, 24, 384), V(128, 768), V(128, 768), V(128, 1152), V(128, 384), V(8, 24, 384), V(2, 12, 384), V(8, 12, 384)]
        + landing_shapes()
        + [D(2), D(2), D(2, 4), D(2, 4, 4), D(2), D(2, 7)],
        compiler_params=pltpu.CompilerParams(collective_id=1, has_side_effects=True, vmem_limit_bytes=big),
    )(out_in, tg_in, xhat, mix, dqkv, u_in, gain, wrows)
    return out.reshape(shape), tg.reshape(shape), qkv_rows, out_rows, gain_rows[:, 0]


def solution(mesh):
    whole = P(None, "tm", "patch", None)
    rows = P("tm", None)
    return jax.shard_map(
        body,
        mesh=mesh,
        in_specs=(whole, P(), P(), P(), whole),
        out_specs=(whole, whole, rows, rows, P("tm")),
        check_vma=False,
    )
```

```python
import functools

import jax
import jax.numpy as jnp
from jax import lax
from jax.experimental import pallas as pl
from jax.experimental.pallas import tpu as pltpu
from jax.sharding import PartitionSpec as P

F32, BF16 = jnp.float32, jnp.bfloat16
MESH = pl.DeviceIdType.MESH


def split(a):
    hi = a.astype(BF16)
    return hi, (a - hi.astype(F32)).astype(BF16)

def dot(a, b, ca=1, cb=0):
    return lax.dot_general(a, b, (((ca,), (cb,)), ((), ())), preferred_element_type=F32)

def rows2(a, b): return jnp.concatenate([a, b], 0)
def cols2(a, b): return jnp.concatenate([a, b], 1)

def product(a_hi, a_lo, b_hi, b_lo, cb=0):
    m = a_hi.shape[0]
    both = dot(rows2(a_hi, a_lo), b_hi, 1, cb)
    return both[:m] + both[m:] + dot(a_hi, b_lo, 1, cb)

def head_pair(x):
    lane = lax.broadcasted_iota(jnp.int32, x.shape, 1)
    first = lane < 64
    return split(rows2(jnp.where(first, x, 0.0), jnp.where(first, 0.0, x)))

def by_heads(x, pair):
    hi, lo = split(x)
    p_hi, p_lo = pair
    return dot(cols2(hi, lo), cols2(p_hi, p_hi), 1, 1) + dot(hi, p_lo, 1, 1)

def mix_heads(x, pair):
    hi, lo = split(x)
    p_hi, p_lo = pair
    both = dot(hi, cols2(p_hi, p_lo))
    return both[:, :128] + both[:, 128:] + dot(lo, p_hi)

def back_heads(x, y):
    hi, lo = split(x.T)
    y_hi, y_lo = split(y)
    both = dot(hi, cols2(y_hi, y_lo))
    r = both[:, :128] + both[:, 128:] + dot(lo, y_hi)
    lane = lax.broadcasted_iota(jnp.int32, (128, 128), 1)
    return jnp.where(lane < 64, r[:128], r[128:])

def prep_weights(w, wh, wl, step):
    for n in range(0, w.shape[1], step):
        hi, lo = split(w[:, n:n + step])
        wh[:, n:n + step] = hi
        wl[:, n:n + step] = lo

def forward(t, gain, wqh, wql, woh, wol, xhat_ref, inv_ref, qkv, probs, mix, out):
    mean = jnp.mean(t, axis=1, keepdims=True)
    cen = t - mean
    inv = lax.rsqrt(jnp.mean(cen * cen, axis=1, keepdims=True) + 1e-5)
    xhat = cen * inv
    xhat_ref[...] = xhat
    inv_ref[...] = jnp.broadcast_to(inv, inv_ref.shape)
    n_hi, n_lo = split(xhat * gain)
    for n in range(0, 2304, 256):
        r = product(n_hi, n_lo, wqh[:, n:n + 256], wql[:, n:n + 256])
        qkv[:, n:n + 256] = r * 0.125 if n < 768 else r
    for p in range(6):
        c = 128 * p
        s = by_heads(qkv[:, c:c + 128], head_pair(qkv[:, 768 + c:768 + c + 128]))
        ps = []
        for h in range(2):
            e = s[:, 128 * h:128 * h + 128]
            e = jnp.exp(e - jnp.max(e, axis=1, keepdims=True))
            ps.append(e / jnp.sum(e, axis=1, keepdims=True))
        pr = cols2(*ps)
        probs[:, 256 * p:256 * p + 256] = pr
        mix[:, c:c + 128] = mix_heads(pr, head_pair(qkv[:, 1536 + c:1536 + c + 128]))
    m_hi, m_lo = split(mix[...])
    for n in range(0, 768, 256):
        out[:, n:n + 256] = t[:, n:n + 256] + product(m_hi, m_lo, woh[:, n:n + 256], wol[:, n:n + 256])

def backward_attn(u, woh, wol, qkv, probs, dmix, dqkv):
    u_hi, u_lo = split(u)
    for n in range(0, 768, 256):
        dmix[:, n:n + 256] = product(u_hi, u_lo, woh[n:n + 256, :], wol[n:n + 256, :], 1)
    for p in range(6):
        c = 128 * p
        do = dmix[:, c:c + 128]
        pr = probs[:, 256 * p:256 * p + 256]
        dqkv[:, 1536 + c:1536 + c + 128] = back_heads(pr, do)
        dp = by_heads(do, head_pair(qkv[:, 1536 + c:1536 + c + 128]))
        ds = []
        for h in range(2):
            a, b = pr[:, 128 * h:128 * h + 128], dp[:, 128 * h:128 * h + 128]
            ds.append(a * (b - jnp.sum(a * b, axis=1, keepdims=True)))
        ds = cols2(*ds)
        dqkv[:, c:c + 128] = 0.125 * mix_heads(ds, head_pair(qkv[:, 768 + c:768 + c + 128]))
        dqkv[:, 768 + c:768 + c + 128] = back_heads(ds, qkv[:, c:c + 128])

def backward_norm(u, gain, wqh, wql, xhat_ref, inv_ref, dqkv, tg):
    d_hi, d_lo = split(dqkv[...])
    for n in range(0, 768, 256):
        tg[:, n:n + 256] = product(d_hi, d_lo, wqh[n:n + 256, :], wql[n:n + 256, :], 1)
    dn = tg[...] * gain
    xhat = xhat_ref[...]
    first = jnp.mean(dn, axis=1, keepdims=True)
    second = jnp.mean(dn * xhat, axis=1, keepdims=True)
    tg[...] = u + inv_ref[:, :1] * (dn - first - xhat * second)

def place():
    return lax.axis_index("tm"), lax.axis_index("patch")


def pack(value, send):
    for i in range(2):
        for c in range(6):
            send[:, 6 * i + c, :] = value[64 * i:64 * i + 64, 128 * c:128 * c + 128]


def unpack(received, store):
    for i in range(2):
        for c in range(6):
            store(i, c, received[:, 6 * i + c, :])


def greet(extra):
    t, q = place()
    barrier = pltpu.get_barrier_semaphore()

    @pl.loop(1, 64)
    def _(k):
        pl.semaphore_signal(barrier, inc=1, device_id=(t ^ k, q), device_id_type=MESH)

    for peer in extra:
        pl.semaphore_signal(barrier, inc=1, device_id=peer, device_id_type=MESH)


def greeted(extra):
    pl.semaphore_wait(pltpu.get_barrier_semaphore(), 63 + len(extra))


def exchange_start(send, received, sems):
    t, q = place()

    @pl.loop(1, 64)
    def _(k):
        peer = lax.rem(t + k, 64)
        pltpu.make_async_remote_copy(
            send.at[peer], received.at[t], sems.at[0], sems.at[1], device_id=(peer, q), device_id_type=MESH
        ).start()

    received[pl.ds(t, 1)] = send[pl.ds(t, 1)]


def exchange_wait(send, received, sems):
    t, q = place()
    all_bytes = pltpu.make_async_remote_copy(
        send.at[pl.ds(0, 63)], received.at[pl.ds(0, 63)], sems.at[0], sems.at[1], device_id=(t ^ 1, q), device_id_type=MESH
    )
    all_bytes.wait_send()
    all_bytes.wait_recv()


def own_rows(w_ref, rows):
    t, _ = place()
    base = pl.multiple_of(t // 2 * 24 + lax.rem(t, 2) * 8, 8)
    wide = w_ref[pl.ds(base, 16), :]
    rows[...] = jnp.where(lax.rem(t, 2) == 0, wide[:12], wide[4:])


def bits():
    t, q = place()
    x, yh, yl = lax.rem(t, 4), lax.rem(t // 4, 2), q // 2
    return {"a": lax.rem(x, 2) ^ (x // 2), "b": x // 2, "c": yl ^ yh, "d": yh}


def partner(dim):
    t, q = place()
    return {"a": (t ^ 1, q), "b": (t ^ 3, q), "c": (t, q ^ 2), "d": (t ^ 4, q ^ 2)}[dim]


DIMS = "abcd"
AXIS = {"a": 0, "c": 1, "d": 3, "b": 4}
PARTS = (0, 1, 4, 5, 2, 3, 6, 7)


def order(part):
    return [DIMS[(part // 2 + s) % 4] for s in range(4)]


def extents(part, step):
    size = [2, 2, 1, 2, 2]
    for dim in order(part)[:step + 1]:
        size[AXIS[dim]] = 1
    return size


def select(part, step, own, other):
    at = [pl.ds(0, 2), pl.ds(0, 2), pl.ds(part, 1), pl.ds(0, 2), pl.ds(0, 2)]
    for s, dim in enumerate(order(part)[:step + 1]):
        bit = own[dim]
        at[AXIS[dim]] = pl.ds(1 - bit if other and s == step else bit, 1)
    return tuple(at)


def reduce_copy(part, step, own, terms, landing, sems):
    return pltpu.make_async_remote_copy(
        terms.at[select(part, step, own, True)],
        landing[step][part],
        sems.at[0, step, part],
        sems.at[1, step, part],
        device_id=partner(order(part)[step]),
        device_id_type=MESH,
    )


def reduce_add(part, step, own, terms, landing):
    at = select(part, step, own, False)
    size = extents(part, step)
    buf = landing[step][part]
    for i in range(size[0]):
        for j in range(size[1]):
            for k in range(size[2]):
                for m in range(size[3]):
                    for n in range(size[4]):
                        idx = tuple(s.start + o for s, o in zip(at, (i, j, k, m, n)))
                        terms[idx] = terms[idx] + buf[i, j, k, m, n]


def landing_shapes():
    return [pltpu.VMEM(tuple(extents(part, step)) + (24, 384), F32) for step in range(4) for part in range(8)]


def group_peers():
    t, q = place()
    return [(t ^ dx, q ^ dq) for dx in (0, 1) for dq in range(4) if dx or dq]


def sibling_copy(src, dst, sems, k):
    t, q = place()
    return pltpu.make_async_remote_copy(src, dst, sems.at[0, k], sems.at[1, k], device_id=(t, q ^ 1), device_id_type=MESH)


def join_left(ref, j, own, theirs):
    hi, lo = split(rows2(own, theirs).T)
    ref[j, :, :256] = hi
    ref[j, :, 256:512] = lo
    ref[j, :, 512:] = hi


def join_right(ref, j, own, theirs):
    hi, lo = split(rows2(own, theirs))
    ref[j, :256] = hi
    ref[j, 256:512] = hi
    ref[j, 512:] = lo


def layer_kernel(
    tok_hbm, up_hbm, g_ref, wq_hbm, wo_hbm,
    o_hbm, g_hbm, p_hbm, w_hbm,
    tok, wq, wo, wrows, up,
    wqh, wql, woh, wol, t_ref, u_ref, out, tg, xhat, inv, qkv, probs, mix, dmix, dqkv,
    send_t, send_u, send_o, send_g, recv_t, recv_u, recv_o, recv_g,
    s_xhat, s_mix, s_dqkv, s_up, left, right, terms, recv_z, own_piece, pieces,
    *rest,
):
    landing = [rest[8 * s:8 * s + 8] for s in range(4)]
    sem_in, sem_t, sem_u, sem_o, sem_g, sem_sib, sem_red, sem_z, sem_p, sem_out = rest[32:]
    t, q = place()
    z, core = t // 8, lax.rem(q, 2)
    own = bits()
    peers = group_peers()
    extra = [p for k, p in enumerate(peers) if k != 3] + [(t ^ 4, q ^ 2)]
    loads = [
        pltpu.make_async_copy(src, dst, sem_in.at[k])
        for k, (src, dst) in enumerate(((tok_hbm, tok), (up_hbm, up), (wq_hbm, wq), (wo_hbm, wo)))
    ]
    for load in loads:
        load.start()
    greet(extra)
    loads[0].wait()
    pack(tok, send_t)
    greeted(extra)
    exchange_start(send_t, recv_t, sem_t)
    loads[1].wait()
    pack(up, send_u)
    exchange_start(send_u, recv_u, sem_u)
    loads[2].wait()
    prep_weights(wq, wqh, wql, 256)
    own_rows(wq, wrows)
    loads[3].wait()
    prep_weights(wo, woh, wol, 256)
    gain = g_ref[...].reshape(1, 768)

    def into(ref):
        def store(i, c, v):
            ref[64 * i:64 * i + 64, 128 * c:128 * c + 128] = v

        return store

    exchange_wait(send_t, recv_t, sem_t)
    unpack(recv_t, into(t_ref))
    forward(t_ref[...], gain, wqh, wql, woh, wol, xhat, inv, qkv, probs, mix, out)
    sib = [sibling_copy(xhat, s_xhat, sem_sib, 0), sibling_copy(mix, s_mix, sem_sib, 1)]
    for copy in sib:
        copy.start()
    pack(out, send_o)
    exchange_start(send_o, recv_o, sem_o)
    for k, (a, b) in enumerate(((xhat, s_xhat), (mix, s_mix))):
        sib[k].wait()
        join_left(left, k, a[...], b[...])
    exchange_wait(send_u, recv_u, sem_u)
    unpack(recv_u, into(u_ref))
    sib_u = sibling_copy(u_ref.at[:, pl.ds(pl.multiple_of((1 - core) * 384, 128), 384)], s_up, sem_sib, 2)
    sib_u.start()
    backward_attn(u_ref[...], woh, wol, qkv, probs, dmix, dqkv)
    sib_d = sibling_copy(dqkv.at[:, pl.ds(pl.multiple_of((1 - core) * 1152, 128), 1152)], s_dqkv, sem_sib, 3)
    sib_d.start()
    backward_norm(u_ref[...], gain, wqh, wql, xhat, inv, dqkv, tg)
    sib_u.wait()
    join_right(right, 3, u_ref[:, pl.ds(pl.multiple_of(core * 384, 128), 384)], s_up[...])
    sib_d.wait()
    for j in range(3):
        col = pl.ds(pl.multiple_of(core * 1152 + 384 * j, 128), 384)
        join_right(right, j, dqkv[:, col], s_dqkv[:, 384 * j:384 * j + 384])

    def block(r, i, j):
        g = 2 * i + j
        v = dot(left[g // 3, 192 * r:192 * r + 192, :], right[g])
        terms[i, j, 2 * r:2 * r + 2] = v.reshape(2, 2, 2, 24, 384)

    def begin(p, step):
        reduce_copy(p, step, own, terms, landing, sem_red).start()

    a, c = own["a"], own["c"]
    both = (0, 1)
    for r, blocks in ((0, [(1 - a, j) for j in both]), (2, [(i, 1 - c) for i in both]), (1, None), (3, None)):
        for i, j in blocks or [(i, j) for i in both for j in both]:
            block(r, i, j)
        begin(2 * r, 0)
        begin(2 * r + 1, 0)
    for j in both:
        block(0, a, j)
    for i in both:
        block(2, i, c)
    pack(tg, send_g)
    exchange_start(send_g, recv_g, sem_g)
    for step in range(4):
        for p in PARTS:
            reduce_copy(p, step, own, terms, landing, sem_red).wait()
            reduce_add(p, step, own, terms, landing)
            if step < 3:
                begin(p, step + 1)
            else:

                @pl.when(z != p)
                def _(p=p):
                    pltpu.make_async_remote_copy(
                        terms.at[a, c, p, own["d"], own["b"]], recv_z.at[z], sem_z.at[0], sem_z.at[1],
                        device_id=(p * 8 + lax.rem(t, 8), q), device_id_type=MESH,
                    ).start()

    recv_z[pl.ds(z, 1)] = terms[a, c, pl.ds(z, 1), own["d"], own["b"]]
    exchange_wait(send_o, recv_o, sem_o)
    exchange_wait(send_g, recv_g, sem_g)
    results = [
        pltpu.make_async_copy(src, dst, sem_out.at[k])
        for k, (src, dst) in enumerate(((recv_o, o_hbm), (recv_g, g_hbm), (wrows, w_hbm), (pieces, p_hbm)))
    ]
    for result in results[:3]:
        result.start()
    every = pltpu.make_async_remote_copy(
        recv_z.at[pl.ds(0, 7)], recv_z.at[pl.ds(0, 7)], sem_z.at[0], sem_z.at[1], device_id=(t ^ 8, q), device_id_type=MESH
    )
    every.wait_send()
    every.wait_recv()
    total = recv_z[0]
    for k in range(1, 8):
        total = total + recv_z[k]
    own_piece[0] = total[:12]
    own_piece[1] = total[12:]
    me = core * 4 + a * 2 + c
    copies = []
    for k, (pt, pq) in enumerate(peers):
        copy = pltpu.make_async_remote_copy(
            own_piece.at[lax.rem(pt, 2)], pieces.at[me], sem_p.at[0, k], sem_p.at[1, k], device_id=(pt, pq), device_id_type=MESH
        )
        copy.start()
        copies.append(copy)
    pieces[pl.ds(me, 1)] = own_piece[pl.ds(lax.rem(t, 2), 1)]
    for copy in copies:
        copy.wait()
    results[3].start()
    for result in results:
        result.wait()


def finish_kernel(recv_o, recv_g, pieces, wrows, g_ref, out, tg, qkv_rows, out_rows, gain_rows):
    t, _ = place()
    lane = lax.broadcasted_iota(jnp.int32, (12, 768), 1)
    row = lax.broadcasted_iota(jnp.int32, (12, 768), 0)
    gain = jnp.sum(jnp.where(lane == row + 12 * t, g_ref[...].reshape(1, 768), 0.0), axis=1, keepdims=True)
    gain_sum = jnp.zeros((12, 1), F32)
    for k in range(8):
        j, c = k % 4, k // 4
        piece = pieces[k]
        if j < 3:
            col = 1152 * c + 384 * j
            qkv_rows[:, col:col + 384] = piece * gain
            gain_sum = gain_sum + jnp.sum(piece * wrows[:, col:col + 384], axis=1, keepdims=True)
        else:
            out_rows[:, 384 * c:384 * c + 384] = piece
    gain_rows[...] = gain_sum.reshape(12)
    for recv, o in ((recv_o, out), (recv_g, tg)):

        def store(i, c, v, o=o):
            o[64 * i:64 * i + 64, 128 * c:128 * c + 128] = v

        unpack(recv, store)


def body(tokens, norm_gain_vector, qkv_weight, out_weight, upstream):
    shape = tokens.shape
    tok, up = tokens.reshape(128, 768), upstream.reshape(128, 768)
    vmem, hbm = pl.BlockSpec(memory_space=pltpu.VMEM), pl.BlockSpec(memory_space=pl.ANY)
    S = lambda *s: jax.ShapeDtypeStruct(s, F32)
    V = lambda *s: pltpu.VMEM(s, F32)
    H = lambda *s: pltpu.VMEM(s, BF16)
    D = lambda *s: pltpu.SemaphoreType.DMA(s)
    rows = V(128, 768)
    pack_buffer = V(64, 12, 128)
    recv_o, recv_g, pieces, wrows = pl.pallas_call(
        layer_kernel,
        out_shape=[S(64, 12, 128), S(64, 12, 128), S(8, 12, 384), S(12, 2304)],
        in_specs=[hbm, hbm, vmem, hbm, hbm],
        out_specs=[hbm] * 4,
        scratch_shapes=[rows, V(768, 2304), V(768, 768), V(12, 2304), rows]
        + [H(768, 2304), H(768, 2304), H(768, 768), H(768, 768)]
        + [rows, rows, rows, rows, rows, V(128, 128), V(128, 2304), V(128, 1536), rows, rows, V(128, 2304)]
        + [pack_buffer] * 8
        + [rows, rows, V(128, 1152), V(128, 384), H(2, 768, 768), H(4, 768, 384)]
        + [V(2, 2, 8, 2, 2, 24, 384), V(8, 24, 384), V(2, 12, 384), V(8, 12, 384)]
        + landing_shapes()
        + [D(4), D(2), D(2), D(2), D(2), D(2, 4), D(2, 4, 8), D(2), D(2, 7), D(4)],
        compiler_params=pltpu.CompilerParams(collective_id=0, has_side_effects=True, vmem_limit_bytes=60 * 2 ** 20),
    )(tok, up, norm_gain_vector, qkv_weight, out_weight)
    out, tg, qkv_rows, out_rows, gain_rows = pl.pallas_call(
        finish_kernel,
        out_shape=[S(128, 768), S(128, 768), S(12, 2304), S(12, 768), S(12)],
        in_specs=[vmem] * 5,
        out_specs=[vmem] * 5,
        compiler_params=pltpu.CompilerParams(vmem_limit_bytes=16 * 2 ** 20),
    )(recv_o, recv_g, pieces, wrows, norm_gain_vector)
    return out.reshape(shape), tg.reshape(shape), qkv_rows, out_rows, gain_rows


def solution(mesh):
    whole = P(None, "tm", "patch", None)
    rows = P("tm", None)
    return jax.shard_map(
        body,
        mesh=mesh,
        in_specs=(whole, P(), P(), P(), whole),
        out_specs=(whole, whole, rows, rows, P("tm")),
        check_vma=False,
    )
```

```python
import functools

import jax
import jax.numpy as jnp
from jax import lax
from jax.experimental import pallas as pl
from jax.experimental.pallas import tpu as pltpu
from jax.sharding import PartitionSpec as P

F32, BF16 = jnp.float32, jnp.bfloat16
MESH = pl.DeviceIdType.MESH


def split(a):
    hi = a.astype(BF16)
    return hi, (a - hi.astype(F32)).astype(BF16)

def dot(a, b, ca=1, cb=0):
    return lax.dot_general(a, b, (((ca,), (cb,)), ((), ())), preferred_element_type=F32)

def rows2(a, b): return jnp.concatenate([a, b], 0)
def cols2(a, b): return jnp.concatenate([a, b], 1)

def product(a_hi, a_lo, b_hi, b_lo, cb=0):
    m = a_hi.shape[0]
    both = dot(rows2(a_hi, a_lo), b_hi, 1, cb)
    return both[:m] + both[m:] + dot(a_hi, b_lo, 1, cb)

def head_pair(x):
    lane = lax.broadcasted_iota(jnp.int32, x.shape, 1)
    first = lane < 64
    return split(rows2(jnp.where(first, x, 0.0), jnp.where(first, 0.0, x)))

def by_heads(x, pair):
    hi, lo = split(x)
    p_hi, p_lo = pair
    return dot(cols2(hi, lo), cols2(p_hi, p_hi), 1, 1) + dot(hi, p_lo, 1, 1)

def mix_heads(x, pair):
    hi, lo = split(x)
    p_hi, p_lo = pair
    both = dot(hi, cols2(p_hi, p_lo))
    return both[:, :128] + both[:, 128:] + dot(lo, p_hi)

def back_heads(x, y):
    hi, lo = split(x.T)
    y_hi, y_lo = split(y)
    both = dot(hi, cols2(y_hi, y_lo))
    r = both[:, :128] + both[:, 128:] + dot(lo, y_hi)
    lane = lax.broadcasted_iota(jnp.int32, (128, 128), 1)
    return jnp.where(lane < 64, r[:128], r[128:])

def prep_weights(w, wh, wl, step):
    for n in range(0, w.shape[1], step):
        hi, lo = split(w[:, n:n + step])
        wh[:, n:n + step] = hi
        wl[:, n:n + step] = lo

def forward(t, gain, wqh, wql, woh, wol, xhat_ref, inv_ref, qkv, probs, mix, out):
    mean = jnp.mean(t, axis=1, keepdims=True)
    cen = t - mean
    inv = lax.rsqrt(jnp.mean(cen * cen, axis=1, keepdims=True) + 1e-5)
    xhat = cen * inv
    xhat_ref[...] = xhat
    inv_ref[...] = jnp.broadcast_to(inv, inv_ref.shape)
    n_hi, n_lo = split(xhat * gain)
    for n in range(0, 2304, 256):
        r = product(n_hi, n_lo, wqh[:, n:n + 256], wql[:, n:n + 256])
        qkv[:, n:n + 256] = r * 0.125 if n < 768 else r
    for p in range(6):
        c = 128 * p
        s = by_heads(qkv[:, c:c + 128], head_pair(qkv[:, 768 + c:768 + c + 128]))
        ps = []
        for h in range(2):
            e = s[:, 128 * h:128 * h + 128]
            e = jnp.exp(e - jnp.max(e, axis=1, keepdims=True))
            ps.append(e / jnp.sum(e, axis=1, keepdims=True))
        pr = cols2(*ps)
        probs[:, 256 * p:256 * p + 256] = pr
        mix[:, c:c + 128] = mix_heads(pr, head_pair(qkv[:, 1536 + c:1536 + c + 128]))
    m_hi, m_lo = split(mix[...])
    for n in range(0, 768, 256):
        out[:, n:n + 256] = t[:, n:n + 256] + product(m_hi, m_lo, woh[:, n:n + 256], wol[:, n:n + 256])

def back_values(u, woh, wol, probs, dmix, dqkv):
    u_hi, u_lo = split(u)
    for n in range(0, 768, 256):
        dmix[:, n:n + 256] = product(u_hi, u_lo, woh[n:n + 256, :], wol[n:n + 256, :], 1)
    for p in range(6):
        c = 128 * p
        dqkv[:, 1536 + c:1536 + c + 128] = back_heads(probs[:, 256 * p:256 * p + 256], dmix[:, c:c + 128])


def back_scores(qkv, probs, dmix, dqkv):
    for p in range(6):
        c = 128 * p
        pr = probs[:, 256 * p:256 * p + 256]
        dp = by_heads(dmix[:, c:c + 128], head_pair(qkv[:, 1536 + c:1536 + c + 128]))
        ds = []
        for h in range(2):
            a, b = pr[:, 128 * h:128 * h + 128], dp[:, 128 * h:128 * h + 128]
            ds.append(a * (b - jnp.sum(a * b, axis=1, keepdims=True)))
        ds = cols2(*ds)
        dqkv[:, c:c + 128] = 0.125 * mix_heads(ds, head_pair(qkv[:, 768 + c:768 + c + 128]))
        dqkv[:, 768 + c:768 + c + 128] = back_heads(ds, qkv[:, c:c + 128])


def backward_norm(u, gain, wqh, wql, xhat_ref, inv_ref, dqkv, tg):
    d_hi, d_lo = split(dqkv[...])
    for n in range(0, 768, 256):
        tg[:, n:n + 256] = product(d_hi, d_lo, wqh[n:n + 256, :], wql[n:n + 256, :], 1)
    dn = tg[...] * gain
    xhat = xhat_ref[...]
    first = jnp.mean(dn, axis=1, keepdims=True)
    second = jnp.mean(dn * xhat, axis=1, keepdims=True)
    tg[...] = u + inv_ref[:, :1] * (dn - first - xhat * second)

def place():
    return lax.axis_index("tm"), lax.axis_index("patch")


def pack(value, send):
    for i in range(2):
        for c in range(6):
            send[:, 6 * i + c, :] = value[64 * i:64 * i + 64, 128 * c:128 * c + 128]


def unpack(received, store):
    for i in range(2):
        for c in range(6):
            store(i, c, received[:, 6 * i + c, :])


def greet(extra):
    t, q = place()
    barrier = pltpu.get_barrier_semaphore()

    @pl.loop(1, 64)
    def _(k):
        pl.semaphore_signal(barrier, inc=1, device_id=(t ^ k, q), device_id_type=MESH)

    for peer in extra:
        pl.semaphore_signal(barrier, inc=1, device_id=peer, device_id_type=MESH)


def greeted(extra):
    pl.semaphore_wait(pltpu.get_barrier_semaphore(), 63 + len(extra))


def exchange_start(send, received, sems):
    t, q = place()

    @pl.loop(1, 64)
    def _(k):
        peer = lax.rem(t + k, 64)
        pltpu.make_async_remote_copy(
            send.at[peer], received.at[t], sems.at[0], sems.at[1], device_id=(peer, q), device_id_type=MESH
        ).start()

    received[pl.ds(t, 1)] = send[pl.ds(t, 1)]


def exchange_wait(send, received, sems):
    t, q = place()
    all_bytes = pltpu.make_async_remote_copy(
        send.at[pl.ds(0, 63)], received.at[pl.ds(0, 63)], sems.at[0], sems.at[1], device_id=(t ^ 1, q), device_id_type=MESH
    )
    all_bytes.wait_send()
    all_bytes.wait_recv()


def own_rows(w_ref, rows):
    t, _ = place()
    base = pl.multiple_of(t // 2 * 24 + lax.rem(t, 2) * 8, 8)
    wide = w_ref[pl.ds(base, 16), :]
    rows[...] = jnp.where(lax.rem(t, 2) == 0, wide[:12], wide[4:])


def bits():
    t, q = place()
    x, yh, yl = lax.rem(t, 4), lax.rem(t // 4, 2), q // 2
    return {"a": lax.rem(x, 2) ^ (x // 2), "b": x // 2, "c": yl ^ yh, "d": yh}


def partner(dim):
    t, q = place()
    return {"a": (t ^ 1, q), "b": (t ^ 3, q), "c": (t, q ^ 2), "d": (t ^ 4, q ^ 2)}[dim]


AXIS = {"a": (0, 1), "c": (1, 0), "d": (3, None), "b": (4, None)}
SUBS = ((0, 0, 256), (0, 256, 128), (1, 0, 256), (1, 256, 128))
PLAN = (
    'value',
    0,
    'scores',
    1,
    2,
    (0, 0),
    3,
    'norm',
    (1, 0),
    (0, 1),
    (2, 0),
    (1, 1),
    (0, 2),
    (3, 0),
    'return',
    (2, 1),
    (1, 2),
    (0, 3),
    (3, 1),
    (2, 2),
    (1, 3),
    (3, 2),
    (2, 3),
    (3, 3),
)


def order(chunk, sub):
    return ["abcd"[(chunk + sub + s) % 4] for s in range(4)]


def extents(chunk, sub, step):
    size = [2, 2, 1, 2, 2]
    for dim in order(chunk, sub)[:step + 1]:
        size[AXIS[dim][0]] = 1
    return size


def select(chunk, sub, step, own, other):
    z0, col, cols = SUBS[sub]
    at = [pl.ds(0, 2), pl.ds(0, 2), pl.ds(z0, 1), pl.ds(0, 2), pl.ds(0, 2)]
    for s, dim in enumerate(order(chunk, sub)[:step + 1]):
        axis, place_in = AXIS[dim]
        bit = own[dim] if place_in is None else own[dim] ^ ((chunk >> place_in) & 1)
        at[axis] = pl.ds(1 - bit if other and s == step else bit, 1)
    return at


def reduce_copy(chunk, sub, step, own, terms, landing, sems):
    z0, col, cols = SUBS[sub]
    return pltpu.make_async_remote_copy(
        terms.at[(chunk, *select(chunk, sub, step, own, True), slice(None), pl.ds(col, cols))],
        landing[step][4 * chunk + sub],
        sems.at[0, step, 4 * chunk + sub],
        sems.at[1, step, 4 * chunk + sub],
        device_id=partner(order(chunk, sub)[step]),
        device_id_type=MESH,
    )


def reduce_add(chunk, sub, step, own, terms, landing):
    z0, col, cols = SUBS[sub]
    at = select(chunk, sub, step, own, False)
    size = extents(chunk, sub, step)
    buf = landing[step][4 * chunk + sub]
    for n in range(size[0] * size[1] * size[3] * size[4]):
        pos, left = [0] * 5, n
        for axis in (4, 3, 1, 0):
            pos[axis], left = left % size[axis], left // size[axis]
        idx = (chunk, *(s.start + o for s, o in zip(at, pos)), slice(None), slice(col, col + cols))
        terms[idx] = terms[idx] + buf[tuple(pos)]


def landing_shapes():
    return [
        pltpu.VMEM(tuple(extents(k, s, step)) + (24, SUBS[s][2]), F32)
        for step in range(4) for k in range(4) for s in range(4)
    ]


def group_peers():
    t, q = place()
    return [(t ^ dx, q ^ dq) for dx in (0, 1) for dq in range(4) if dx or dq]


def sibling_copy(src, dst, sems, k):
    t, q = place()
    return pltpu.make_async_remote_copy(src, dst, sems.at[0, k], sems.at[1, k], device_id=(t, q ^ 1), device_id_type=MESH)


def join_left(ref, j, own, theirs):
    hi, lo = split(rows2(own, theirs).T)
    ref[j, :, :256] = hi
    ref[j, :, 256:512] = lo
    ref[j, :, 512:] = hi


def join_right(ref, j, own, theirs):
    hi, lo = split(rows2(own, theirs))
    ref[j, :256] = hi
    ref[j, 256:512] = hi
    ref[j, 512:] = lo


def layer_kernel(
    tok_hbm, up_hbm, g_ref, wq_hbm, wo_hbm,
    o_hbm, g_hbm, p_hbm, w_hbm,
    tok, wq, wo, wrows, up,
    wqh, wql, woh, wol, t_ref, u_ref, out, tg, xhat, inv, qkv, probs, mix, dmix, dqkv,
    send_t, send_u, send_o, send_g, recv_t, recv_u, recv_o, recv_g,
    s_xhat, s_mix, s_u, s_v, s_k, s_q, left, right, terms, recv_z, own_piece, pieces,
    *rest,
):
    landing = [rest[16 * s:16 * s + 16] for s in range(4)]
    sem_in, sem_t, sem_u, sem_o, sem_g, sem_sib, sem_red, sem_z, sem_p, sem_out = rest[64:]
    t, q = place()
    z, core = t // 8, lax.rem(q, 2)
    own = bits()
    peers = group_peers()
    extra = [p for k, p in enumerate(peers) if k != 3] + [(t ^ 4, q ^ 2)]
    loads = [
        pltpu.make_async_copy(src, dst, sem_in.at[k])
        for k, (src, dst) in enumerate(((tok_hbm, tok), (up_hbm, up), (wq_hbm, wq), (wo_hbm, wo)))
    ]
    loads[0].start()
    loads[1].start()
    greet(extra)
    loads[0].wait()
    pack(tok, send_t)
    greeted(extra)
    exchange_start(send_t, recv_t, sem_t)
    loads[1].wait()
    pack(up, send_u)
    exchange_start(send_u, recv_u, sem_u)
    loads[2].start()
    loads[3].start()
    loads[2].wait()
    prep_weights(wq, wqh, wql, 256)
    own_rows(wq, wrows)
    loads[3].wait()
    prep_weights(wo, woh, wol, 256)
    gain = g_ref[...].reshape(1, 768)

    def into(ref):
        def store(i, c, v):
            ref[64 * i:64 * i + 64, 128 * c:128 * c + 128] = v

        return store

    exchange_wait(send_t, recv_t, sem_t)
    unpack(recv_t, into(t_ref))
    forward(t_ref[...], gain, wqh, wql, woh, wol, xhat, inv, qkv, probs, mix, out)
    sib = [sibling_copy(xhat, s_xhat, sem_sib, 0), sibling_copy(mix, s_mix, sem_sib, 1)]
    for copy in sib:
        copy.start()
    pack(out, send_o)
    exchange_start(send_o, recv_o, sem_o)
    for k, (a, b) in enumerate(((xhat, s_xhat), (mix, s_mix))):
        sib[k].wait()
        join_left(left, k, a[...], b[...])
    exchange_wait(send_u, recv_u, sem_u)
    unpack(recv_u, into(u_ref))

    def half(ref, start, k):
        return ref.at[:, pl.ds(pl.multiple_of(start + k * 384, 128), 384)]

    sources = ((u_ref, 0, s_u), (dqkv, 1536, s_v), (dqkv, 768, s_k), (dqkv, 0, s_q))

    def share(k):
        ref, start, landed = sources[k]
        return sibling_copy(half(ref, start, 1 - core), landed, sem_sib, 2 + k)

    def chunk(k):
        share(k).wait()
        ref, start, landed = sources[k]
        join_right(right, k, half(ref, start, core)[...], landed[...])
        for r in range(4):
            v = dot(left[1 if k == 0 else 0, 192 * r:192 * r + 192, :], right[k])
            terms[k, r // 2, r % 2] = v.reshape(2, 2, 2, 24, 384)
        for s in range(4):
            reduce_copy(k, s, 0, own, terms, landing, sem_red).start()

    a, c = own["a"], own["c"]

    def arrive(k, step):
        for s in range(4):
            reduce_copy(k, s, step, own, terms, landing, sem_red).wait()
            reduce_add(k, s, step, own, terms, landing)
            if step < 3:
                reduce_copy(k, s, step + 1, own, terms, landing, sem_red).start()
        if step < 3:
            return
        z2, z1 = a ^ (k >> 1), c ^ (k & 1)
        for z0 in range(2):
            to = 4 * z2 + 2 * z1 + z0
            block = terms.at[k, z2, z1, z0, own["d"], own["b"]]

            @pl.when(z != to)
            def _(to=to, block=block):
                pltpu.make_async_remote_copy(
                    block, recv_z.at[z], sem_z.at[0], sem_z.at[1],
                    device_id=(to * 8 + lax.rem(t, 8), q), device_id_type=MESH,
                ).start()

            @pl.when(z == to)
            def _(block=block):
                recv_z[pl.ds(z, 1)] = block[...].reshape(1, 24, 384)

    share(0).start()
    for task in PLAN:
        if task == "value":
            back_values(u_ref[...], woh, wol, probs, dmix, dqkv)
            share(1).start()
        elif task == "scores":
            back_scores(qkv, probs, dmix, dqkv)
            share(2).start()
            share(3).start()
        elif task == "norm":
            backward_norm(u_ref[...], gain, wqh, wql, xhat, inv, dqkv, tg)
        elif task == "return":
            pack(tg, send_g)
            exchange_start(send_g, recv_g, sem_g)
        elif isinstance(task, int):
            chunk(task)
        else:
            arrive(*task)

    exchange_wait(send_o, recv_o, sem_o)
    exchange_wait(send_g, recv_g, sem_g)
    results = [
        pltpu.make_async_copy(src, dst, sem_out.at[k])
        for k, (src, dst) in enumerate(((recv_o, o_hbm), (recv_g, g_hbm), (wrows, w_hbm), (pieces, p_hbm)))
    ]
    for result in results[:3]:
        result.start()
    every = pltpu.make_async_remote_copy(
        recv_z.at[pl.ds(0, 7)], recv_z.at[pl.ds(0, 7)], sem_z.at[0], sem_z.at[1], device_id=(t ^ 8, q), device_id_type=MESH
    )
    every.wait_send()
    every.wait_recv()
    total = recv_z[0]
    for k in range(1, 8):
        total = total + recv_z[k]
    own_piece[0] = total[:12]
    own_piece[1] = total[12:]
    me = core * 4 + (a ^ (z // 4)) * 2 + (c ^ lax.rem(z // 2, 2))
    copies = []
    for k, (pt, pq) in enumerate(peers):
        copy = pltpu.make_async_remote_copy(
            own_piece.at[lax.rem(pt, 2)], pieces.at[me], sem_p.at[0, k], sem_p.at[1, k], device_id=(pt, pq), device_id_type=MESH
        )
        copy.start()
        copies.append(copy)
    pieces[pl.ds(me, 1)] = own_piece[pl.ds(lax.rem(t, 2), 1)]
    for copy in copies:
        copy.wait()
    results[3].start()
    for result in results:
        result.wait()


def finish_kernel(recv_o, recv_g, pieces, wrows, g_ref, out, tg, qkv_rows, out_rows, gain_rows):
    t, _ = place()
    lane = lax.broadcasted_iota(jnp.int32, (12, 768), 1)
    row = lax.broadcasted_iota(jnp.int32, (12, 768), 0)
    gain = jnp.sum(jnp.where(lane == row + 12 * t, g_ref[...].reshape(1, 768), 0.0), axis=1, keepdims=True)
    gain_sum = jnp.zeros((12, 1), F32)
    for k in range(8):
        chunk, c = k % 4, k // 4
        piece = pieces[k]
        if chunk:
            col = 768 * (3 - chunk) + 384 * c
            qkv_rows[:, col:col + 384] = piece * gain
            gain_sum = gain_sum + jnp.sum(piece * wrows[:, col:col + 384], axis=1, keepdims=True)
        else:
            out_rows[:, 384 * c:384 * c + 384] = piece
    gain_rows[...] = gain_sum.reshape(12)
    for recv, o in ((recv_o, out), (recv_g, tg)):

        def store(i, c, v, o=o):
            o[64 * i:64 * i + 64, 128 * c:128 * c + 128] = v

        unpack(recv, store)


def body(tokens, norm_gain_vector, qkv_weight, out_weight, upstream):
    shape = tokens.shape
    tok, up = tokens.reshape(128, 768), upstream.reshape(128, 768)
    vmem, hbm = pl.BlockSpec(memory_space=pltpu.VMEM), pl.BlockSpec(memory_space=pl.ANY)
    S = lambda *s: jax.ShapeDtypeStruct(s, F32)
    V = lambda *s: pltpu.VMEM(s, F32)
    H = lambda *s: pltpu.VMEM(s, BF16)
    D = lambda *s: pltpu.SemaphoreType.DMA(s)
    rows = V(128, 768)
    pack_buffer = V(64, 12, 128)
    recv_o, recv_g, pieces, wrows = pl.pallas_call(
        layer_kernel,
        out_shape=[S(64, 12, 128), S(64, 12, 128), S(8, 12, 384), S(12, 2304)],
        in_specs=[hbm, hbm, vmem, hbm, hbm],
        out_specs=[hbm] * 4,
        scratch_shapes=[rows, V(768, 2304), V(768, 768), V(12, 2304), rows]
        + [H(768, 2304), H(768, 2304), H(768, 768), H(768, 768)]
        + [rows, rows, rows, rows, rows, V(128, 128), V(128, 2304), V(128, 1536), rows, rows, V(128, 2304)]
        + [pack_buffer] * 8
        + [rows, rows, V(128, 384), V(128, 384), V(128, 384), V(128, 384), H(2, 768, 768), H(4, 768, 384)]
        + [V(4, 2, 2, 2, 2, 2, 24, 384), V(8, 24, 384), V(2, 12, 384), V(8, 12, 384)]
        + landing_shapes()
        + [D(4), D(2), D(2), D(2), D(2), D(2, 6), D(2, 4, 16), D(2), D(2, 7), D(4)],
        compiler_params=pltpu.CompilerParams(collective_id=0, has_side_effects=True, vmem_limit_bytes=60 * 2 ** 20),
    )(tok, up, norm_gain_vector, qkv_weight, out_weight)
    out, tg, qkv_rows, out_rows, gain_rows = pl.pallas_call(
        finish_kernel,
        out_shape=[S(128, 768), S(128, 768), S(12, 2304), S(12, 768), S(12)],
        in_specs=[vmem] * 5,
        out_specs=[vmem] * 5,
        compiler_params=pltpu.CompilerParams(vmem_limit_bytes=60 * 2 ** 20),
    )(recv_o, recv_g, pieces, wrows, norm_gain_vector)
    return out.reshape(shape), tg.reshape(shape), qkv_rows, out_rows, gain_rows


def solution(mesh):
    whole = P(None, "tm", "patch", None)
    rows = P("tm", None)
    return jax.shard_map(
        body,
        mesh=mesh,
        in_specs=(whole, P(), P(), P(), whole),
        out_specs=(whole, whole, rows, rows, P("tm")),
        check_vma=False,
    )
```

```python
import functools

import jax
import jax.numpy as jnp
from jax import lax
from jax.experimental import pallas as pl
from jax.experimental.pallas import tpu as pltpu
from jax.sharding import PartitionSpec as P

F32, BF16 = jnp.float32, jnp.bfloat16
MESH = pl.DeviceIdType.MESH


def split(a):
    hi = a.astype(BF16)
    return hi, (a - hi.astype(F32)).astype(BF16)

def dot(a, b, ca=1, cb=0):
    return lax.dot_general(a, b, (((ca,), (cb,)), ((), ())), preferred_element_type=F32)

def rows2(a, b): return jnp.concatenate([a, b], 0)
def cols2(a, b): return jnp.concatenate([a, b], 1)

def product(a_hi, a_lo, b_hi, b_lo, cb=0):
    m = a_hi.shape[0]
    both = dot(rows2(a_hi, a_lo), b_hi, 1, cb)
    return both[:m] + both[m:] + dot(a_hi, b_lo, 1, cb)

def head_pair(x):
    lane = lax.broadcasted_iota(jnp.int32, x.shape, 1)
    first = lane < 64
    return split(rows2(jnp.where(first, x, 0.0), jnp.where(first, 0.0, x)))

def by_heads(x, pair):
    hi, lo = split(x)
    p_hi, p_lo = pair
    return dot(cols2(hi, lo), cols2(p_hi, p_hi), 1, 1) + dot(hi, p_lo, 1, 1)

def mix_heads(x, pair):
    hi, lo = split(x)
    p_hi, p_lo = pair
    both = dot(hi, cols2(p_hi, p_lo))
    return both[:, :128] + both[:, 128:] + dot(lo, p_hi)

def back_heads(x, y):
    hi, lo = split(x.T)
    y_hi, y_lo = split(y)
    both = dot(hi, cols2(y_hi, y_lo))
    r = both[:, :128] + both[:, 128:] + dot(lo, y_hi)
    lane = lax.broadcasted_iota(jnp.int32, (128, 128), 1)
    return jnp.where(lane < 64, r[:128], r[128:])

def prep_weights(w, wh, wl, step):
    for n in range(0, w.shape[1], step):
        hi, lo = split(w[:, n:n + step])
        wh[:, n:n + step] = hi
        wl[:, n:n + step] = lo

def forward(t, gain, wqh, wql, woh, wol, xhat_ref, inv_ref, qkv, probs, mix, out):
    mean = jnp.mean(t, axis=1, keepdims=True)
    cen = t - mean
    inv = lax.rsqrt(jnp.mean(cen * cen, axis=1, keepdims=True) + 1e-5)
    xhat = cen * inv
    xhat_ref[...] = xhat
    inv_ref[...] = jnp.broadcast_to(inv, inv_ref.shape)
    n_hi, n_lo = split(xhat * gain)
    for n in range(0, 2304, 256):
        r = product(n_hi, n_lo, wqh[:, n:n + 256], wql[:, n:n + 256])
        qkv[:, n:n + 256] = r * 0.125 if n < 768 else r
    for p in range(6):
        c = 128 * p
        s = by_heads(qkv[:, c:c + 128], head_pair(qkv[:, 768 + c:768 + c + 128]))
        ps = []
        for h in range(2):
            e = s[:, 128 * h:128 * h + 128]
            e = jnp.exp(e - jnp.max(e, axis=1, keepdims=True))
            ps.append(e / jnp.sum(e, axis=1, keepdims=True))
        pr = cols2(*ps)
        probs[:, 256 * p:256 * p + 256] = pr
        mix[:, c:c + 128] = mix_heads(pr, head_pair(qkv[:, 1536 + c:1536 + c + 128]))
    m_hi, m_lo = split(mix[...])
    for n in range(0, 768, 256):
        out[:, n:n + 256] = t[:, n:n + 256] + product(m_hi, m_lo, woh[:, n:n + 256], wol[:, n:n + 256])

def back_values(u, woh, wol, probs, dmix, dqkv):
    u_hi, u_lo = split(u)
    for n in range(0, 768, 256):
        dmix[:, n:n + 256] = product(u_hi, u_lo, woh[n:n + 256, :], wol[n:n + 256, :], 1)
    for p in range(6):
        c = 128 * p
        dqkv[:, 1536 + c:1536 + c + 128] = back_heads(probs[:, 256 * p:256 * p + 256], dmix[:, c:c + 128])


def back_scores(qkv, probs, dmix, dqkv):
    for p in range(6):
        c = 128 * p
        pr = probs[:, 256 * p:256 * p + 256]
        dp = by_heads(dmix[:, c:c + 128], head_pair(qkv[:, 1536 + c:1536 + c + 128]))
        ds = []
        for h in range(2):
            a, b = pr[:, 128 * h:128 * h + 128], dp[:, 128 * h:128 * h + 128]
            ds.append(a * (b - jnp.sum(a * b, axis=1, keepdims=True)))
        ds = cols2(*ds)
        dqkv[:, c:c + 128] = 0.125 * mix_heads(ds, head_pair(qkv[:, 768 + c:768 + c + 128]))
        dqkv[:, 768 + c:768 + c + 128] = back_heads(ds, qkv[:, c:c + 128])


def backward_norm(u, gain, wqh, wql, xhat_ref, inv_ref, dqkv, tg):
    d_hi, d_lo = split(dqkv[...])
    for n in range(0, 768, 256):
        tg[:, n:n + 256] = product(d_hi, d_lo, wqh[n:n + 256, :], wql[n:n + 256, :], 1)
    dn = tg[...] * gain
    xhat = xhat_ref[...]
    first = jnp.mean(dn, axis=1, keepdims=True)
    second = jnp.mean(dn * xhat, axis=1, keepdims=True)
    tg[...] = u + inv_ref[:, :1] * (dn - first - xhat * second)

def place():
    return lax.axis_index("tm"), lax.axis_index("patch")


def far_first():
    steps = [(dz, dy, dx) for dz in range(8) for dy in range(2) for dx in range(4)][1:]
    return sorted(steps, key=lambda v: -(min(v[0], 8 - v[0]) + 2 * v[1] + min(v[2], 4 - v[2])))


def others():
    t, _ = place()
    z, y, x = t // 8, lax.rem(t // 4, 2), lax.rem(t, 4)
    return [(lax.rem(z + dz, 8) * 2 + (y ^ dy)) * 4 + lax.rem(x + dx, 4) for dz, dy, dx in far_first()]


def pack(value, send):
    for i in range(2):
        for c in range(6):
            send[:, 6 * i + c, :] = value[64 * i:64 * i + 64, 128 * c:128 * c + 128]


def unpack(received, store):
    for i in range(2):
        for c in range(6):
            store(i, c, received[:, 6 * i + c, :])


def greet(extra):
    t, q = place()
    barrier = pltpu.get_barrier_semaphore()

    for peer in others():
        pl.semaphore_signal(barrier, inc=1, device_id=(peer, q), device_id_type=MESH)

    for peer in extra:
        pl.semaphore_signal(barrier, inc=1, device_id=peer, device_id_type=MESH)


def greeted(extra):
    pl.semaphore_wait(pltpu.get_barrier_semaphore(), 63 + len(extra))


def exchange_start(send, received, sems):
    t, q = place()

    for peer in others():
        pltpu.make_async_remote_copy(
            send.at[peer], received.at[t], sems.at[0], sems.at[1], device_id=(peer, q), device_id_type=MESH
        ).start()

    received[pl.ds(t, 1)] = send[pl.ds(t, 1)]


def exchange_wait(send, received, sems):
    t, q = place()
    all_bytes = pltpu.make_async_remote_copy(
        send.at[pl.ds(0, 63)], received.at[pl.ds(0, 63)], sems.at[0], sems.at[1], device_id=(t ^ 1, q), device_id_type=MESH
    )
    all_bytes.wait_send()
    all_bytes.wait_recv()


def own_rows(w_ref, rows):
    t, _ = place()
    base = pl.multiple_of(t // 2 * 24 + lax.rem(t, 2) * 8, 8)
    wide = w_ref[pl.ds(base, 16), :]
    rows[...] = jnp.where(lax.rem(t, 2) == 0, wide[:12], wide[4:])


def bits():
    t, q = place()
    x, yh, yl, z0 = lax.rem(t, 4), lax.rem(t // 4, 2), q // 2, lax.rem(t // 8, 2)
    return {"a": lax.rem(x, 2) ^ (x // 2), "b": x // 2, "c": yl ^ yh, "d": yh, "e": z0, "f": z0}


def partner(dim):
    t, q = place()
    if dim == "f":
        return (lax.rem(t + jnp.where(lax.rem(t // 8, 2) == 0, 56, 8), 64), q)
    return {"a": (t ^ 1, q), "b": (t ^ 3, q), "c": (t, q ^ 2), "d": (t ^ 4, q ^ 2), "e": (t ^ 8, q)}[dim]


AXIS = {"a": (0, 1), "c": (1, 0), "d": (3, None), "b": (4, None), "e": (2, None), "f": (2, None)}
SUBS = (
    ((None, 0, 128, "eabcd"), (None, 128, 128, "fbcda"), (0, 256, 128, "cdab"), (1, 256, 128, "dabc")),
    ((None, 0, 128, "ecdab"), (None, 128, 128, "fdabc"), (0, 256, 128, "abcd"), (1, 256, 128, "bcda")),
    ((0, 0, 256, "cdab"), (0, 256, 128, "dabc"), (1, 0, 256, "abcd"), (1, 256, 128, "bcda")),
    ((0, 0, 256, "dabc"), (0, 256, 128, "abcd"), (1, 0, 256, "bcda"), (1, 256, 128, "cdab")),
)
BY_Z = (0, 1)
PLAN = (
    'value',
    0,
    'scores',
    1,
    2,
    (0, 0),
    'norm',
    (1, 0),
    (0, 1),
    (2, 0),
    (1, 1),
    (0, 2),
    (3, 0),
    (2, 1),
    (1, 2),
    'return',
    (0, 3),
    (3, 1),
    (2, 2),
    (1, 3),
    (0, 4),
    (3, 2),
    (1, 4),
    (2, 3),
    (3, 3),
)


def order(chunk, sub):
    return SUBS[chunk][sub][3]


def extents(chunk, sub, step):
    size = [2, 2, 2 if SUBS[chunk][sub][0] is None else 1, 2, 2]
    for dim in order(chunk, sub)[:step + 1]:
        size[AXIS[dim][0]] = 1
    return size


def select(chunk, sub, step, own, other):
    z0 = SUBS[chunk][sub][0]
    at = [pl.ds(0, 2), pl.ds(0, 2), pl.ds(0, 2) if z0 is None else pl.ds(z0, 1), pl.ds(0, 2), pl.ds(0, 2)]
    for s, dim in enumerate(order(chunk, sub)[:step + 1]):
        axis, place_in = AXIS[dim]
        bit = own[dim] if place_in is None else own[dim] ^ ((chunk >> place_in) & 1)
        at[axis] = pl.ds(1 - bit if other and s == step else bit, 1)
    return at


def reduce_copy(chunk, sub, step, own, terms, landing, sems):
    _, col, cols, dims = SUBS[chunk][sub]
    return pltpu.make_async_remote_copy(
        terms.at[(chunk, *select(chunk, sub, step, own, True), slice(None), pl.ds(col, cols))],
        landing[chunk, sub, step],
        sems.at[0, step, 4 * chunk + sub],
        sems.at[1, step, 4 * chunk + sub],
        device_id=partner(dims[step]),
        device_id_type=MESH,
    )


def reduce_add(chunk, sub, step, own, terms, landing):
    _, col, cols, _ = SUBS[chunk][sub]
    at = select(chunk, sub, step, own, False)
    size = extents(chunk, sub, step)
    buf = landing[chunk, sub, step]
    for n in range(size[0] * size[1] * size[2] * size[3] * size[4]):
        pos, left = [0] * 5, n
        for axis in (4, 3, 2, 1, 0):
            pos[axis], left = left % size[axis], left // size[axis]
        idx = (chunk, *(s.start + o for s, o in zip(at, pos)), slice(None), slice(col, col + cols))
        terms[idx] = terms[idx] + buf[tuple(pos)]


def landings():
    return [(k, s, step) for k in range(4) for s in range(4) for step in range(len(order(k, s)))]


def landing_shapes():
    return [pltpu.VMEM(tuple(extents(*key)) + (24, SUBS[key[0]][key[1]][2]), F32) for key in landings()]


def group_peers():
    t, q = place()
    return [(t ^ dx, q ^ dq) for dx in (0, 1) for dq in range(4) if dx or dq]


def sibling_copy(src, dst, sems, k):
    t, q = place()
    return pltpu.make_async_remote_copy(src, dst, sems.at[0, k], sems.at[1, k], device_id=(t, q ^ 1), device_id_type=MESH)


def join_left(ref, j, own, theirs):
    hi, lo = split(rows2(own, theirs).T)
    ref[j, :, :256] = hi
    ref[j, :, 256:512] = lo
    ref[j, :, 512:] = hi


def join_right(ref, j, own, theirs):
    hi, lo = split(rows2(own, theirs))
    ref[j, :256] = hi
    ref[j, 256:512] = hi
    ref[j, 512:] = lo


def layer_kernel(
    tok_hbm, up_hbm, g_ref, wq_hbm, wo_hbm,
    o_hbm, g_hbm, p_hbm, w_hbm,
    tok, wq, wo, wrows, up,
    wqh, wql, woh, wol, t_ref, u_ref, out, tg, xhat, inv, qkv, probs, mix, dmix, dqkv,
    send_t, send_u, send_o, send_g, recv_t, recv_u, recv_o, recv_g,
    s_xhat, s_mix, s_u, s_v, s_k, s_q, left, right, terms, recv_z, own_piece, pieces,
    *rest,
):
    landing = dict(zip(landings(), rest))
    sem_in, sem_t, sem_u, sem_o, sem_g, sem_sib, sem_red, sem_z, sem_p, sem_out = rest[len(landing):]
    t, q = place()
    z, core = t // 8, lax.rem(q, 2)
    own = bits()
    peers = group_peers()
    extra = [p for k, p in enumerate(peers) if k != 3] + [(t ^ 4, q ^ 2)]
    loads = [
        pltpu.make_async_copy(src, dst, sem_in.at[k])
        for k, (src, dst) in enumerate(((tok_hbm, tok), (up_hbm, up), (wq_hbm, wq), (wo_hbm, wo)))
    ]
    loads[0].start()
    loads[1].start()
    recv_z[...] = jnp.zeros_like(recv_z)
    greet(extra)
    loads[0].wait()
    pack(tok, send_t)
    greeted(extra)
    exchange_start(send_t, recv_t, sem_t)
    loads[1].wait()
    pack(up, send_u)
    exchange_start(send_u, recv_u, sem_u)
    loads[2].start()
    loads[3].start()
    loads[2].wait()
    prep_weights(wq, wqh, wql, 256)
    own_rows(wq, wrows)
    loads[3].wait()
    prep_weights(wo, woh, wol, 256)
    gain = g_ref[...].reshape(1, 768)

    def into(ref):
        def store(i, c, v):
            ref[64 * i:64 * i + 64, 128 * c:128 * c + 128] = v

        return store

    exchange_wait(send_t, recv_t, sem_t)
    unpack(recv_t, into(t_ref))
    forward(t_ref[...], gain, wqh, wql, woh, wol, xhat, inv, qkv, probs, mix, out)
    sib = [sibling_copy(xhat, s_xhat, sem_sib, 0), sibling_copy(mix, s_mix, sem_sib, 1)]
    for copy in sib:
        copy.start()
    pack(out, send_o)
    exchange_start(send_o, recv_o, sem_o)
    for k, (a, b) in enumerate(((xhat, s_xhat), (mix, s_mix))):
        sib[k].wait()
        join_left(left, k, a[...], b[...])
    exchange_wait(send_u, recv_u, sem_u)
    unpack(recv_u, into(u_ref))

    def half(ref, start, k):
        return ref.at[:, pl.ds(pl.multiple_of(start + k * 384, 128), 384)]

    sources = ((u_ref, 0, s_u), (dqkv, 1536, s_v), (dqkv, 768, s_k), (dqkv, 0, s_q))

    def share(k):
        ref, start, landed = sources[k]
        return sibling_copy(half(ref, start, 1 - core), landed, sem_sib, 2 + k)

    def chunk(*ks):
        for k in ks:
            share(k).wait()
            ref, start, landed = sources[k]
            join_right(right, k, half(ref, start, core)[...], landed[...])
        for r in range(4):
            rows = left[1 if ks[0] == 0 else 0, 192 * r:192 * r + 192, :]
            both = dot(rows, jnp.concatenate([right[k] for k in ks], 1))
            for n, k in enumerate(ks):
                terms[k, r // 2, r % 2] = both[:, 384 * n:384 * n + 384].reshape(2, 2, 2, 24, 384)
        for k in ks:
            for s in range(4):
                reduce_copy(k, s, 0, own, terms, landing, sem_red).start()

    a, c = own["a"], own["c"]

    def arrive(k, step):
        for s in range(4):
            steps = len(order(k, s))
            if step >= steps:
                continue
            reduce_copy(k, s, step, own, terms, landing, sem_red).wait()
            reduce_add(k, s, step, own, terms, landing)
            if step < steps - 1:
                reduce_copy(k, s, step + 1, own, terms, landing, sem_red).start()
        if step < max(len(order(k, s)) for s in range(4)) - 1:
            return
        z2, z1 = a ^ (k >> 1), c ^ (k & 1)
        for z0 in range(2):
            to = 4 * z2 + 2 * z1 + z0
            block = terms.at[k, z2, z1, z0, own["d"], own["b"]]
            far = {"device_id": (to * 8 + lax.rem(t, 8), q), "device_id_type": MESH}

            @pl.when((z != to) & (own["e"] == z0))
            def _(block=block, far=far):
                pltpu.make_async_remote_copy(block, recv_z.at[z], sem_z.at[0], sem_z.at[3], **far).start()

            @pl.when(own["e"] != z0)
            def _(block=block, far=far):
                if k in BY_Z:
                    last = pl.ds(256, 128)
                    pltpu.make_async_remote_copy(
                        block.at[:, last], recv_z.at[z, :, last], sem_z.at[1], sem_z.at[4], **far
                    ).start()
                else:
                    pltpu.make_async_remote_copy(block, recv_z.at[z], sem_z.at[2], sem_z.at[4], **far).start()

            @pl.when(z == to)
            def _(block=block):
                recv_z[pl.ds(z, 1)] = block[...].reshape(1, 24, 384)

    share(0).start()
    for task in PLAN:
        if task == "value":
            back_values(u_ref[...], woh, wol, probs, dmix, dqkv)
            share(1).start()
        elif task == "scores":
            back_scores(qkv, probs, dmix, dqkv)
            share(2).start()
            share(3).start()
        elif task == "norm":
            backward_norm(u_ref[...], gain, wqh, wql, xhat, inv, dqkv, tg)
        elif task == "return":
            pack(tg, send_g)
            exchange_start(send_g, recv_g, sem_g)
        elif isinstance(task, int):
            chunk(*((2, 3) if task == 2 else (task,)))
        else:
            arrive(*task)

    exchange_wait(send_o, recv_o, sem_o)
    exchange_wait(send_g, recv_g, sem_g)
    results = [
        pltpu.make_async_copy(src, dst, sem_out.at[k])
        for k, (src, dst) in enumerate(((recv_o, o_hbm), (recv_g, g_hbm), (wrows, w_hbm), (pieces, p_hbm)))
    ]
    for result in results[:3]:
        result.start()
    held = (a ^ (z // 4)) * 2 + (c ^ lax.rem(z // 2, 2))

    def landed(n, cols, k):
        ref = recv_z.at[pl.ds(0, n), :, pl.ds(0, cols)]
        return pltpu.make_async_copy(ref, ref, sem_z.at[k])

    landed(3, 384, 0).wait()
    landed(2, 128, 1).wait()
    landed(2, 384, 2).wait()
    landed(3, 384, 3).wait()

    @pl.when(held < 2)
    def _():
        landed(4, 128, 4).wait()

    @pl.when(held >= 2)
    def _():
        landed(4, 384, 4).wait()

    total = recv_z[0]
    for k in range(1, 8):
        total = total + recv_z[k]
    own_piece[0] = total[:12]
    own_piece[1] = total[12:]
    me = core * 4 + held
    copies = []
    for k, (pt, pq) in enumerate(peers):
        copy = pltpu.make_async_remote_copy(
            own_piece.at[lax.rem(pt, 2)], pieces.at[me], sem_p.at[0, k], sem_p.at[1, k], device_id=(pt, pq), device_id_type=MESH
        )
        copy.start()
        copies.append(copy)
    pieces[pl.ds(me, 1)] = own_piece[pl.ds(lax.rem(t, 2), 1)]
    for copy in copies:
        copy.wait()
    results[3].start()
    for result in results:
        result.wait()


def finish_kernel(recv_o, recv_g, pieces, wrows, g_ref, out, tg, qkv_rows, out_rows, gain_rows):
    t, _ = place()
    lane = lax.broadcasted_iota(jnp.int32, (12, 768), 1)
    row = lax.broadcasted_iota(jnp.int32, (12, 768), 0)
    gain = jnp.sum(jnp.where(lane == row + 12 * t, g_ref[...].reshape(1, 768), 0.0), axis=1, keepdims=True)
    gain_sum = jnp.zeros((12, 1), F32)
    for k in range(8):
        chunk, c = k % 4, k // 4
        piece = pieces[k]
        if chunk:
            col = 768 * (3 - chunk) + 384 * c
            qkv_rows[:, col:col + 384] = piece * gain
            gain_sum = gain_sum + jnp.sum(piece * wrows[:, col:col + 384], axis=1, keepdims=True)
        else:
            out_rows[:, 384 * c:384 * c + 384] = piece
    gain_rows[...] = gain_sum.reshape(12)
    for recv, o in ((recv_o, out), (recv_g, tg)):

        def store(i, c, v, o=o):
            o[64 * i:64 * i + 64, 128 * c:128 * c + 128] = v

        unpack(recv, store)


def body(tokens, norm_gain_vector, qkv_weight, out_weight, upstream):
    shape = tokens.shape
    tok, up = tokens.reshape(128, 768), upstream.reshape(128, 768)
    vmem, hbm = pl.BlockSpec(memory_space=pltpu.VMEM), pl.BlockSpec(memory_space=pl.ANY)
    S = lambda *s: jax.ShapeDtypeStruct(s, F32)
    V = lambda *s: pltpu.VMEM(s, F32)
    H = lambda *s: pltpu.VMEM(s, BF16)
    D = lambda *s: pltpu.SemaphoreType.DMA(s)
    rows = V(128, 768)
    pack_buffer = V(64, 12, 128)
    recv_o, recv_g, pieces, wrows = pl.pallas_call(
        layer_kernel,
        out_shape=[S(64, 12, 128), S(64, 12, 128), S(8, 12, 384), S(12, 2304)],
        in_specs=[hbm, hbm, vmem, hbm, hbm],
        out_specs=[hbm] * 4,
        scratch_shapes=[rows, V(768, 2304), V(768, 768), V(12, 2304), rows]
        + [H(768, 2304), H(768, 2304), H(768, 768), H(768, 768)]
        + [rows, rows, rows, rows, rows, V(128, 128), V(128, 2304), V(128, 1536), rows, rows, V(128, 2304)]
        + [pack_buffer] * 8
        + [rows, rows, V(128, 384), V(128, 384), V(128, 384), V(128, 384), H(2, 768, 768), H(4, 768, 384)]
        + [V(4, 2, 2, 2, 2, 2, 24, 384), V(8, 24, 384), V(2, 12, 384), V(8, 12, 384)]
        + landing_shapes()
        + [D(4), D(2), D(2), D(2), D(2), D(2, 6), D(2, 5, 16), D(5), D(2, 7), D(4)],
        compiler_params=pltpu.CompilerParams(collective_id=0, has_side_effects=True, vmem_limit_bytes=60 * 2 ** 20),
    )(tok, up, norm_gain_vector, qkv_weight, out_weight)
    out, tg, qkv_rows, out_rows, gain_rows = pl.pallas_call(
        finish_kernel,
        out_shape=[S(128, 768), S(128, 768), S(12, 2304), S(12, 768), S(12)],
        in_specs=[vmem] * 5,
        out_specs=[vmem] * 5,
        compiler_params=pltpu.CompilerParams(vmem_limit_bytes=60 * 2 ** 20),
    )(recv_o, recv_g, pieces, wrows, norm_gain_vector)
    return out.reshape(shape), tg.reshape(shape), qkv_rows, out_rows, gain_rows


def solution(mesh):
    whole = P(None, "tm", "patch", None)
    rows = P("tm", None)
    return jax.shard_map(
        body,
        mesh=mesh,
        in_specs=(whole, P(), P(), P(), whole),
        out_specs=(whole, whole, rows, rows, P("tm")),
        check_vma=False,
    )
```

```python
import functools

import jax
import jax.numpy as jnp
from jax import lax
from jax.experimental import pallas as pl
from jax.experimental.pallas import tpu as pltpu
from jax.sharding import PartitionSpec as P

F32, BF16 = jnp.float32, jnp.bfloat16
MESH = pl.DeviceIdType.MESH


def split(a):
    hi = a.astype(BF16)
    return hi, (a - hi.astype(F32)).astype(BF16)

def dot(a, b, ca=1, cb=0):
    return lax.dot_general(a, b, (((ca,), (cb,)), ((), ())), preferred_element_type=F32)

def rows2(a, b): return jnp.concatenate([a, b], 0)
def cols2(a, b): return jnp.concatenate([a, b], 1)

def product(a_hi, a_lo, b_hi, b_lo, cb=0):
    m = a_hi.shape[0]
    both = dot(rows2(a_hi, a_lo), b_hi, 1, cb)
    return both[:m] + both[m:] + dot(a_hi, b_lo, 1, cb)

def head_pair(x):
    lane = lax.broadcasted_iota(jnp.int32, x.shape, 1)
    first = lane < 64
    return split(rows2(jnp.where(first, x, 0.0), jnp.where(first, 0.0, x)))

def by_heads(x, pair):
    hi, lo = split(x)
    p_hi, p_lo = pair
    return dot(cols2(hi, lo), cols2(p_hi, p_hi), 1, 1) + dot(hi, p_lo, 1, 1)

def mix_heads(x, pair):
    hi, lo = split(x)
    p_hi, p_lo = pair
    both = dot(hi, cols2(p_hi, p_lo))
    return both[:, :128] + both[:, 128:] + dot(lo, p_hi)

def back_heads(x, y):
    hi, lo = split(x.T)
    y_hi, y_lo = split(y)
    both = dot(hi, cols2(y_hi, y_lo))
    r = both[:, :128] + both[:, 128:] + dot(lo, y_hi)
    lane = lax.broadcasted_iota(jnp.int32, (128, 128), 1)
    return jnp.where(lane < 64, r[:128], r[128:])

def prep_weights(w, wh, wl, step):
    for n in range(0, w.shape[1], step):
        hi, lo = split(w[:, n:n + step])
        wh[:, n:n + step] = hi
        wl[:, n:n + step] = lo

def forward(t, gain, wqh, wql, woh, wol, xhat_ref, inv_ref, qkv, probs, mix, out):
    mean = jnp.mean(t, axis=1, keepdims=True)
    cen = t - mean
    inv = lax.rsqrt(jnp.mean(cen * cen, axis=1, keepdims=True) + 1e-5)
    xhat = cen * inv
    xhat_ref[...] = xhat
    inv_ref[...] = jnp.broadcast_to(inv, inv_ref.shape)
    n_hi, n_lo = split(xhat * gain)
    for n in range(0, 2304, 256):
        r = product(n_hi, n_lo, wqh[:, n:n + 256], wql[:, n:n + 256])
        qkv[:, n:n + 256] = r * 0.125 if n < 768 else r
    for p in range(6):
        c = 128 * p
        s = by_heads(qkv[:, c:c + 128], head_pair(qkv[:, 768 + c:768 + c + 128]))
        ps = []
        for h in range(2):
            e = s[:, 128 * h:128 * h + 128]
            e = jnp.exp(e - jnp.max(e, axis=1, keepdims=True))
            ps.append(e / jnp.sum(e, axis=1, keepdims=True))
        pr = cols2(*ps)
        probs[:, 256 * p:256 * p + 256] = pr
        mix[:, c:c + 128] = mix_heads(pr, head_pair(qkv[:, 1536 + c:1536 + c + 128]))
    m_hi, m_lo = split(mix[...])
    for n in range(0, 768, 256):
        out[:, n:n + 256] = t[:, n:n + 256] + product(m_hi, m_lo, woh[:, n:n + 256], wol[:, n:n + 256])

def back_values(u, woh, wol, probs, dmix, dqkv):
    u_hi, u_lo = split(u)
    for n in range(0, 768, 256):
        dmix[:, n:n + 256] = product(u_hi, u_lo, woh[n:n + 256, :], wol[n:n + 256, :], 1)
    for p in range(6):
        c = 128 * p
        dqkv[:, 1536 + c:1536 + c + 128] = back_heads(probs[:, 256 * p:256 * p + 256], dmix[:, c:c + 128])


def back_scores(qkv, probs, dmix, dqkv):
    for p in range(6):
        c = 128 * p
        pr = probs[:, 256 * p:256 * p + 256]
        dp = by_heads(dmix[:, c:c + 128], head_pair(qkv[:, 1536 + c:1536 + c + 128]))
        ds = []
        for h in range(2):
            a, b = pr[:, 128 * h:128 * h + 128], dp[:, 128 * h:128 * h + 128]
            ds.append(a * (b - jnp.sum(a * b, axis=1, keepdims=True)))
        ds = cols2(*ds)
        dqkv[:, c:c + 128] = 0.125 * mix_heads(ds, head_pair(qkv[:, 768 + c:768 + c + 128]))
        dqkv[:, 768 + c:768 + c + 128] = back_heads(ds, qkv[:, c:c + 128])


def backward_norm(u, gain, wqh, wql, xhat_ref, inv_ref, dqkv, tg):
    d_hi, d_lo = split(dqkv[...])
    for n in range(0, 768, 256):
        tg[:, n:n + 256] = product(d_hi, d_lo, wqh[n:n + 256, :], wql[n:n + 256, :], 1)
    dn = tg[...] * gain
    xhat = xhat_ref[...]
    first = jnp.mean(dn, axis=1, keepdims=True)
    second = jnp.mean(dn * xhat, axis=1, keepdims=True)
    tg[...] = u + inv_ref[:, :1] * (dn - first - xhat * second)

def place():
    return lax.axis_index("tm"), lax.axis_index("patch")


def far_first():
    steps = [(dz, dy, dx) for dz in range(8) for dy in range(2) for dx in range(4)][1:]
    return sorted(steps, key=lambda v: -(min(v[0], 8 - v[0]) + 2 * v[1] + min(v[2], 4 - v[2])))


def others():
    t, _ = place()
    z, y, x = t // 8, lax.rem(t // 4, 2), lax.rem(t, 4)
    return [(lax.rem(z + dz, 8) * 2 + (y ^ dy)) * 4 + lax.rem(x + dx, 4) for dz, dy, dx in far_first()]


def pack(value, send):
    for i in range(2):
        for c in range(6):
            send[:, 6 * i + c, :] = value[64 * i:64 * i + 64, 128 * c:128 * c + 128]


def unpack(received, store):
    for i in range(2):
        for c in range(6):
            store(i, c, received[:, 6 * i + c, :])


def greet(extra):
    t, q = place()
    barrier = pltpu.get_barrier_semaphore()

    for peer in others():
        pl.semaphore_signal(barrier, inc=1, device_id=(peer, q), device_id_type=MESH)

    for peer in extra:
        pl.semaphore_signal(barrier, inc=1, device_id=peer, device_id_type=MESH)


def greeted(extra):
    pl.semaphore_wait(pltpu.get_barrier_semaphore(), 63 + len(extra))


def exchange_start(send, received, sems):
    t, q = place()

    for peer in others():
        pltpu.make_async_remote_copy(
            send.at[peer], received.at[t], sems.at[0], sems.at[1], device_id=(peer, q), device_id_type=MESH
        ).start()

    received[pl.ds(t, 1)] = send[pl.ds(t, 1)]


def exchange_wait(send, received, sems):
    t, q = place()
    all_bytes = pltpu.make_async_remote_copy(
        send.at[pl.ds(0, 63)], received.at[pl.ds(0, 63)], sems.at[0], sems.at[1], device_id=(t ^ 1, q), device_id_type=MESH
    )
    all_bytes.wait_send()
    all_bytes.wait_recv()


def own_rows(w_ref, rows):
    t, _ = place()
    base = pl.multiple_of(t // 2 * 24 + lax.rem(t, 2) * 8, 8)
    wide = w_ref[pl.ds(base, 16), :]
    rows[...] = jnp.where(lax.rem(t, 2) == 0, wide[:12], wide[4:])


def bits():
    t, q = place()
    x, yh, yl, z0 = lax.rem(t, 4), lax.rem(t // 4, 2), q // 2, lax.rem(t // 8, 2)
    return {"a": lax.rem(x, 2) ^ (x // 2), "b": x // 2, "c": yl ^ yh, "d": yh, "e": z0, "f": z0}


def partner(dim):
    t, q = place()
    if dim == "f":
        return (lax.rem(t + jnp.where(lax.rem(t // 8, 2) == 0, 56, 8), 64), q)
    return {"a": (t ^ 1, q), "b": (t ^ 3, q), "c": (t, q ^ 2), "d": (t ^ 4, q ^ 2), "e": (t ^ 8, q)}[dim]


AXIS = {"a": (0, 1), "c": (1, 0), "d": (3, None), "b": (4, None), "e": (2, None), "f": (2, None)}
SUBS = (
    ((None, 0, 128, "eabcd"), (None, 128, 128, "fbcda"), (0, 256, 128, "cdab"), (1, 256, 128, "dabc")),
    ((None, 0, 128, "ecdab"), (None, 128, 128, "fdabc"), (0, 256, 128, "abcd"), (1, 256, 128, "bcda")),
    ((0, 0, 256, "cdab"), (0, 256, 128, "dabc"), (1, 0, 256, "abcd"), (1, 256, 128, "bcda")),
    ((0, 0, 256, "dabc"), (0, 256, 128, "abcd"), (1, 0, 256, "bcda"), (1, 256, 128, "cdab")),
)
BY_Z = (0, 1)
PLAN = (
    'value',
    0,
    'scores',
    1,
    2,
    (0, 0),
    (1, 0),
    'norm',
    (0, 1),
    (2, 0),
    (1, 1),
    (0, 2),
    (3, 0),
    (2, 1),
    (1, 2),
    'return',
    'take',
    (0, 3),
    (3, 1),
    (2, 2),
    (1, 3),
    (0, 4),
    (3, 2),
    (1, 4),
    (2, 3),
    (3, 3),
)


def order(chunk, sub):
    return SUBS[chunk][sub][3]


def extents(chunk, sub, step):
    size = [2, 2, 2 if SUBS[chunk][sub][0] is None else 1, 2, 2]
    for dim in order(chunk, sub)[:step + 1]:
        size[AXIS[dim][0]] = 1
    return size


def select(chunk, sub, step, own, other):
    z0 = SUBS[chunk][sub][0]
    at = [pl.ds(0, 2), pl.ds(0, 2), pl.ds(0, 2) if z0 is None else pl.ds(z0, 1), pl.ds(0, 2), pl.ds(0, 2)]
    for s, dim in enumerate(order(chunk, sub)[:step + 1]):
        axis, place_in = AXIS[dim]
        bit = own[dim] if place_in is None else own[dim] ^ ((chunk >> place_in) & 1)
        at[axis] = pl.ds(1 - bit if other and s == step else bit, 1)
    return at


def reduce_copy(chunk, sub, step, own, terms, landing, sems):
    _, col, cols, dims = SUBS[chunk][sub]
    return pltpu.make_async_remote_copy(
        terms.at[(chunk, *select(chunk, sub, step, own, True), slice(None), pl.ds(col, cols))],
        landing[chunk, sub, step],
        sems.at[0, step, 4 * chunk + sub],
        sems.at[1, step, 4 * chunk + sub],
        device_id=partner(dims[step]),
        device_id_type=MESH,
    )


def reduce_add(chunk, sub, step, own, terms, landing):
    _, col, cols, _ = SUBS[chunk][sub]
    at = select(chunk, sub, step, own, False)
    size = extents(chunk, sub, step)
    buf = landing[chunk, sub, step]
    for n in range(size[0] * size[1] * size[2] * size[3] * size[4]):
        pos, left = [0] * 5, n
        for axis in (4, 3, 2, 1, 0):
            pos[axis], left = left % size[axis], left // size[axis]
        idx = (chunk, *(s.start + o for s, o in zip(at, pos)), slice(None), slice(col, col + cols))
        terms[idx] = terms[idx] + buf[tuple(pos)]


def landings():
    return [(k, s, step) for k in range(4) for s in range(4) for step in range(len(order(k, s)))]


def landing_shapes():
    return [pltpu.VMEM(tuple(extents(*key)) + (24, SUBS[key[0]][key[1]][2]), F32) for key in landings()]


def group_peers():
    t, q = place()
    return [(t ^ dx, q ^ dq) for dx in (1, 0) for dq in (3, 2, 1, 0) if dx or dq]


def sibling_copy(src, dst, sems, k):
    t, q = place()
    return pltpu.make_async_remote_copy(src, dst, sems.at[0, k], sems.at[1, k], device_id=(t, q ^ 1), device_id_type=MESH)


def join_left(ref, j, own, theirs):
    hi, lo = split(rows2(own, theirs).T)
    ref[j, :, :256] = hi
    ref[j, :, 256:512] = lo
    ref[j, :, 512:] = hi


def join_right(ref, j, own, theirs):
    hi, lo = split(rows2(own, theirs))
    ref[j, :256] = hi
    ref[j, 256:512] = hi
    ref[j, 512:] = lo


def layer_kernel(
    tok_hbm, up_hbm, g_ref, wq_hbm, wo_hbm,
    o_hbm, g_hbm, p_hbm, w_hbm,
    tok, wq, wo, wrows, up,
    wqh, wql, woh, wol, t_ref, u_ref, out, tg, xhat, inv, qkv, probs, mix, dmix, dqkv,
    send_t, send_u, send_o, send_g, recv_t, recv_u, recv_o, recv_g,
    s_xhat, s_mix, s_u, s_v, s_k, s_q, left, right, terms, recv_z, own_piece, pieces,
    *rest,
):
    landing = dict(zip(landings(), rest))
    sem_in, sem_t, sem_u, sem_o, sem_g, sem_sib, sem_red, sem_z, sem_p, sem_out = rest[len(landing):]
    t, q = place()
    z, core = t // 8, lax.rem(q, 2)
    own = bits()
    peers = group_peers()
    extra = [(pt, pq) for pt, pq in peers[:3] + peers[4:]] + [(t ^ 4, q ^ 2)]
    loads = [
        pltpu.make_async_copy(src, dst, sem_in.at[k])
        for k, (src, dst) in enumerate(((tok_hbm, tok), (up_hbm, up), (wq_hbm, wq), (wo_hbm, wo)))
    ]
    loads[0].start()
    loads[1].start()
    recv_z[...] = jnp.zeros_like(recv_z)
    greet(extra)
    loads[0].wait()
    pack(tok, send_t)
    greeted(extra)
    exchange_start(send_t, recv_t, sem_t)
    loads[1].wait()
    pack(up, send_u)
    exchange_start(send_u, recv_u, sem_u)
    loads[2].start()
    loads[3].start()
    loads[2].wait()
    prep_weights(wq, wqh, wql, 256)
    own_rows(wq, wrows)
    loads[3].wait()
    prep_weights(wo, woh, wol, 256)
    gain = g_ref[...].reshape(1, 768)

    def into(ref):
        def store(i, c, v):
            ref[64 * i:64 * i + 64, 128 * c:128 * c + 128] = v

        return store

    exchange_wait(send_t, recv_t, sem_t)
    unpack(recv_t, into(t_ref))
    forward(t_ref[...], gain, wqh, wql, woh, wol, xhat, inv, qkv, probs, mix, out)
    sib = [sibling_copy(xhat, s_xhat, sem_sib, 0), sibling_copy(mix, s_mix, sem_sib, 1)]
    for copy in sib:
        copy.start()
    pack(out, send_o)
    exchange_start(send_o, recv_o, sem_o)
    for k, (a, b) in enumerate(((xhat, s_xhat), (mix, s_mix))):
        sib[k].wait()
        join_left(left, k, a[...], b[...])
    exchange_wait(send_u, recv_u, sem_u)
    unpack(recv_u, into(u_ref))

    def half(ref, start, k):
        return ref.at[:, pl.ds(pl.multiple_of(start + k * 384, 128), 384)]

    sources = ((u_ref, 0, s_u), (dqkv, 1536, s_v), (dqkv, 768, s_k), (dqkv, 0, s_q))

    def share(k):
        ref, start, landed = sources[k]
        return sibling_copy(half(ref, start, 1 - core), landed, sem_sib, 2 + k)

    def chunk(*ks):
        for k in ks:
            share(k).wait()
            ref, start, landed = sources[k]
            join_right(right, k, half(ref, start, core)[...], landed[...])
        for r in range(4):
            rows = left[1 if ks[0] == 0 else 0, 192 * r:192 * r + 192, :]
            both = dot(rows, jnp.concatenate([right[k] for k in ks], 1))
            for n, k in enumerate(ks):
                terms[k, r // 2, r % 2] = both[:, 384 * n:384 * n + 384].reshape(2, 2, 2, 24, 384)
        for k in ks:
            for s in range(4):
                reduce_copy(k, s, 0, own, terms, landing, sem_red).start()

    a, c = own["a"], own["c"]

    def arrive(k, step):
        for s in (range(4) if k in BY_Z else (1, 3, 0, 2)):
            steps = len(order(k, s))
            if step >= steps:
                continue
            reduce_copy(k, s, step, own, terms, landing, sem_red).wait()
            reduce_add(k, s, step, own, terms, landing)
            if step < steps - 1:
                reduce_copy(k, s, step + 1, own, terms, landing, sem_red).start()
        if step < max(len(order(k, s)) for s in range(4)) - 1:
            return
        z2, z1 = a ^ (k >> 1), c ^ (k & 1)
        for z0 in range(2):
            to = 4 * z2 + 2 * z1 + z0
            block = terms.at[k, z2, z1, z0, own["d"], own["b"]]
            far = {"device_id": (to * 8 + lax.rem(t, 8), q), "device_id_type": MESH}

            @pl.when((z != to) & (own["e"] == z0))
            def _(block=block, far=far):
                pltpu.make_async_remote_copy(block, recv_z.at[z], sem_z.at[0], sem_z.at[3], **far).start()

            @pl.when(own["e"] != z0)
            def _(block=block, far=far):
                if k in BY_Z:
                    last = pl.ds(256, 128)
                    pltpu.make_async_remote_copy(
                        block.at[:, last], recv_z.at[z, :, last], sem_z.at[1], sem_z.at[4], **far
                    ).start()
                else:
                    pltpu.make_async_remote_copy(block, recv_z.at[z], sem_z.at[2], sem_z.at[4], **far).start()

            @pl.when(z == to)
            def _(block=block):
                recv_z[pl.ds(z, 1)] = block[...].reshape(1, 24, 384)

    results = [
        pltpu.make_async_copy(src, dst, sem_out.at[k])
        for k, (src, dst) in enumerate(((out, o_hbm), (tg, g_hbm), (wrows, w_hbm), (pieces, p_hbm)))
    ]
    share(0).start()
    for task in PLAN:
        if task == "value":
            back_values(u_ref[...], woh, wol, probs, dmix, dqkv)
            share(1).start()
        elif task == "scores":
            back_scores(qkv, probs, dmix, dqkv)
            share(2).start()
            share(3).start()
        elif task == "norm":
            backward_norm(u_ref[...], gain, wqh, wql, xhat, inv, dqkv, tg)
        elif task == "take":
            exchange_wait(send_o, recv_o, sem_o)
            unpack(recv_o, into(out))
            results[0].start()
            results[2].start()
        elif task == "return":
            pack(tg, send_g)
            exchange_start(send_g, recv_g, sem_g)
        elif isinstance(task, int):
            chunk(*((2, 3) if task == 2 else (task,)))
        else:
            arrive(*task)

    exchange_wait(send_g, recv_g, sem_g)
    unpack(recv_g, into(tg))
    results[1].start()
    held = (a ^ (z // 4)) * 2 + (c ^ lax.rem(z // 2, 2))

    def landed(n, cols, k):
        ref = recv_z.at[pl.ds(0, n), :, pl.ds(0, cols)]
        return pltpu.make_async_copy(ref, ref, sem_z.at[k])

    landed(3, 384, 0).wait()
    landed(2, 128, 1).wait()
    landed(2, 384, 2).wait()
    landed(3, 384, 3).wait()

    @pl.when(held < 2)
    def _():
        landed(4, 128, 4).wait()

    @pl.when(held >= 2)
    def _():
        landed(4, 384, 4).wait()

    total = recv_z[0]
    for k in range(1, 8):
        total = total + recv_z[k]
    own_piece[0] = total[:12]
    own_piece[1] = total[12:]
    me = core * 4 + held
    copies = []
    for k, (pt, pq) in enumerate(peers):
        copy = pltpu.make_async_remote_copy(
            own_piece.at[lax.rem(pt, 2)], pieces.at[me], sem_p.at[0, k], sem_p.at[1, k], device_id=(pt, pq), device_id_type=MESH
        )
        copy.start()
        copies.append(copy)
    pieces[pl.ds(me, 1)] = own_piece[pl.ds(lax.rem(t, 2), 1)]
    for copy in copies:
        copy.wait()
    results[3].start()
    for result in results:
        result.wait()


def finish_kernel(
    o_hbm, g_hbm, p_hbm, w_hbm, gain_hbm, out, tg, qkv_out, out_out, gain_out,
    o_ref, g_ref, pieces, wrows, gain_ref, qkv_rows, out_rows, gain_rows, sems,
):
    t, _ = place()
    pairs = ((p_hbm, pieces), (w_hbm, wrows), (gain_hbm, gain_ref), (o_hbm, o_ref), (g_hbm, g_ref))
    loads = [pltpu.make_async_copy(src, dst, sems.at[k]) for k, (src, dst) in enumerate(pairs)]
    pairs = ((qkv_rows, qkv_out), (out_rows, out_out), (gain_rows, gain_out), (o_ref, out), (g_ref, tg))
    stores = [pltpu.make_async_copy(src, dst, sems.at[5 + k]) for k, (src, dst) in enumerate(pairs)]
    for load in loads:
        load.start()
    for load in loads[:3]:
        load.wait()
    lane = lax.broadcasted_iota(jnp.int32, (12, 768), 1)
    row = lax.broadcasted_iota(jnp.int32, (12, 768), 0)
    gain = jnp.sum(jnp.where(lane == row + 12 * t, gain_ref[...].reshape(1, 768), 0.0), axis=1, keepdims=True)
    gain_sum = jnp.zeros((12, 1), F32)
    for k in range(8):
        chunk, c = k % 4, k // 4
        piece = pieces[k]
        if chunk:
            col = 768 * (3 - chunk) + 384 * c
            qkv_rows[:, col:col + 384] = piece * gain
            gain_sum = gain_sum + jnp.sum(piece * wrows[:, col:col + 384], axis=1, keepdims=True)
        else:
            out_rows[:, 384 * c:384 * c + 384] = piece
    gain_rows[...] = gain_sum.reshape(12)
    for store in stores[:3]:
        store.start()
    for load, store in zip(loads[3:], stores[3:]):
        load.wait()
        store.start()
    for store in stores:
        store.wait()


def body(tokens, norm_gain_vector, qkv_weight, out_weight, upstream):
    shape = tokens.shape
    tok, up = tokens.reshape(128, 768), upstream.reshape(128, 768)
    vmem, hbm = pl.BlockSpec(memory_space=pltpu.VMEM), pl.BlockSpec(memory_space=pl.ANY)
    S = lambda *s: jax.ShapeDtypeStruct(s, F32)
    V = lambda *s: pltpu.VMEM(s, F32)
    H = lambda *s: pltpu.VMEM(s, BF16)
    D = lambda *s: pltpu.SemaphoreType.DMA(s)
    rows = V(128, 768)
    pack_buffer = V(64, 12, 128)
    out_in, tg_in, pieces, wrows = pl.pallas_call(
        layer_kernel,
        out_shape=[S(128, 768), S(128, 768), S(8, 12, 384), S(12, 2304)],
        in_specs=[hbm, hbm, vmem, hbm, hbm],
        out_specs=[hbm] * 4,
        scratch_shapes=[rows, V(768, 2304), V(768, 768), V(12, 2304), rows]
        + [H(768, 2304), H(768, 2304), H(768, 768), H(768, 768)]
        + [rows, rows, rows, rows, rows, V(128, 128), V(128, 2304), V(128, 1536), rows, rows, V(128, 2304)]
        + [pack_buffer] * 8
        + [rows, rows, V(128, 384), V(128, 384), V(128, 384), V(128, 384), H(2, 768, 768), H(4, 768, 384)]
        + [V(4, 2, 2, 2, 2, 2, 24, 384), V(8, 24, 384), V(2, 12, 384), V(8, 12, 384)]
        + landing_shapes()
        + [D(4), D(2), D(2), D(2), D(2), D(2, 6), D(2, 5, 16), D(5), D(2, 7), D(4)],
        compiler_params=pltpu.CompilerParams(collective_id=0, has_side_effects=True, vmem_limit_bytes=60 * 2 ** 20),
    )(tok, up, norm_gain_vector, qkv_weight, out_weight)
    out, tg, qkv_rows, out_rows, gain_rows = pl.pallas_call(
        finish_kernel,
        out_shape=[S(128, 768), S(128, 768), S(12, 2304), S(12, 768), S(12)],
        in_specs=[hbm] * 5,
        out_specs=[hbm] * 5,
        scratch_shapes=[rows, rows, V(8, 12, 384), V(12, 2304), V(768), V(12, 2304), V(12, 768), V(12), D(10)],
        compiler_params=pltpu.CompilerParams(vmem_limit_bytes=60 * 2 ** 20),
    )(out_in, tg_in, pieces, wrows, norm_gain_vector)
    return out.reshape(shape), tg.reshape(shape), qkv_rows, out_rows, gain_rows


def solution(mesh):
    whole = P(None, "tm", "patch", None)
    rows = P("tm", None)
    return jax.shard_map(
        body,
        mesh=mesh,
        in_specs=(whole, P(), P(), P(), whole),
        out_specs=(whole, whole, rows, rows, P("tm")),
        check_vma=False,
    )
```

```python
import functools

import jax
import jax.numpy as jnp
from jax import lax
from jax.experimental import pallas as pl
from jax.experimental.pallas import tpu as pltpu
from jax.sharding import PartitionSpec as P

F32, BF16 = jnp.float32, jnp.bfloat16
MESH = pl.DeviceIdType.MESH


def split(a):
    hi = a.astype(BF16)
    return hi, (a - hi.astype(F32)).astype(BF16)

def dot(a, b, ca=1, cb=0):
    return lax.dot_general(a, b, (((ca,), (cb,)), ((), ())), preferred_element_type=F32)

def rows2(a, b): return jnp.concatenate([a, b], 0)
def cols2(a, b): return jnp.concatenate([a, b], 1)

def product(a_hi, a_lo, b_hi, b_lo, cb=0):
    m = a_hi.shape[0]
    both = dot(rows2(a_hi, a_lo), b_hi, 1, cb)
    return both[:m] + both[m:] + dot(a_hi, b_lo, 1, cb)

def head_pair(x):
    lane = lax.broadcasted_iota(jnp.int32, x.shape, 1)
    first = lane < 64
    return split(rows2(jnp.where(first, x, 0.0), jnp.where(first, 0.0, x)))

def by_heads(x, pair):
    hi, lo = split(x)
    p_hi, p_lo = pair
    return dot(cols2(hi, lo), cols2(p_hi, p_hi), 1, 1) + dot(hi, p_lo, 1, 1)

def mix_heads(x, pair):
    hi, lo = split(x)
    p_hi, p_lo = pair
    both = dot(hi, cols2(p_hi, p_lo))
    return both[:, :128] + both[:, 128:] + dot(lo, p_hi)

def back_heads(x, y):
    hi, lo = split(x.T)
    y_hi, y_lo = split(y)
    both = dot(hi, cols2(y_hi, y_lo))
    r = both[:, :128] + both[:, 128:] + dot(lo, y_hi)
    lane = lax.broadcasted_iota(jnp.int32, (128, 128), 1)
    return jnp.where(lane < 64, r[:128], r[128:])

def prep_weights(w, wh, wl, step):
    for n in range(0, w.shape[1], step):
        hi, lo = split(w[:, n:n + step])
        wh[:, n:n + step] = hi
        wl[:, n:n + step] = lo

def forward(t, gain, wqh, wql, woh, wol, xhat_ref, inv_ref, qkv, probs, mix, out):
    mean = jnp.mean(t, axis=1, keepdims=True)
    cen = t - mean
    inv = lax.rsqrt(jnp.mean(cen * cen, axis=1, keepdims=True) + 1e-5)
    xhat = cen * inv
    xhat_ref[...] = xhat
    inv_ref[...] = jnp.broadcast_to(inv, inv_ref.shape)
    n_hi, n_lo = split(xhat * gain)
    for n in range(0, 2304, 256):
        r = product(n_hi, n_lo, wqh[:, n:n + 256], wql[:, n:n + 256])
        qkv[:, n:n + 256] = r * 0.125 if n < 768 else r
    for p in range(6):
        c = 128 * p
        s = by_heads(qkv[:, c:c + 128], head_pair(qkv[:, 768 + c:768 + c + 128]))
        ps = []
        for h in range(2):
            e = s[:, 128 * h:128 * h + 128]
            e = jnp.exp(e - jnp.max(e, axis=1, keepdims=True))
            ps.append(e / jnp.sum(e, axis=1, keepdims=True))
        pr = cols2(*ps)
        probs[:, 256 * p:256 * p + 256] = pr
        mix[:, c:c + 128] = mix_heads(pr, head_pair(qkv[:, 1536 + c:1536 + c + 128]))
    m_hi, m_lo = split(mix[...])
    for n in range(0, 768, 256):
        out[:, n:n + 256] = t[:, n:n + 256] + product(m_hi, m_lo, woh[:, n:n + 256], wol[:, n:n + 256])

def back_values(u, woh, wol, probs, dmix, dqkv):
    u_hi, u_lo = split(u)
    for n in range(0, 768, 256):
        dmix[:, n:n + 256] = product(u_hi, u_lo, woh[n:n + 256, :], wol[n:n + 256, :], 1)
    for p in range(6):
        c = 128 * p
        dqkv[:, 1536 + c:1536 + c + 128] = back_heads(probs[:, 256 * p:256 * p + 256], dmix[:, c:c + 128])


def back_scores(qkv, probs, dmix, dqkv):
    for p in range(6):
        c = 128 * p
        pr = probs[:, 256 * p:256 * p + 256]
        dp = by_heads(dmix[:, c:c + 128], head_pair(qkv[:, 1536 + c:1536 + c + 128]))
        ds = []
        for h in range(2):
            a, b = pr[:, 128 * h:128 * h + 128], dp[:, 128 * h:128 * h + 128]
            ds.append(a * (b - jnp.sum(a * b, axis=1, keepdims=True)))
        ds = cols2(*ds)
        dqkv[:, c:c + 128] = 0.125 * mix_heads(ds, head_pair(qkv[:, 768 + c:768 + c + 128]))
        dqkv[:, 768 + c:768 + c + 128] = back_heads(ds, qkv[:, c:c + 128])


def backward_norm(u, gain, wqh, wql, xhat_ref, inv_ref, dqkv, tg):
    d_hi, d_lo = split(dqkv[...])
    for n in range(0, 768, 256):
        tg[:, n:n + 256] = product(d_hi, d_lo, wqh[n:n + 256, :], wql[n:n + 256, :], 1)
    dn = tg[...] * gain
    xhat = xhat_ref[...]
    first = jnp.mean(dn, axis=1, keepdims=True)
    second = jnp.mean(dn * xhat, axis=1, keepdims=True)
    tg[...] = u + inv_ref[:, :1] * (dn - first - xhat * second)

def place():
    return lax.axis_index("tm"), lax.axis_index("patch")


def far_first():
    steps = [(dz, dy, dx) for dz in range(8) for dy in range(2) for dx in range(4)][1:]
    return sorted(steps, key=lambda v: -(min(v[0], 8 - v[0]) + 2 * v[1] + min(v[2], 4 - v[2])))


def others():
    t, _ = place()
    z, y, x = t // 8, lax.rem(t // 4, 2), lax.rem(t, 4)
    return [(lax.rem(z + dz, 8) * 2 + (y ^ dy)) * 4 + lax.rem(x + dx, 4) for dz, dy, dx in far_first()]


def pack(value, send):
    for i in range(2):
        for c in range(6):
            send[:, 6 * i + c, :] = value[64 * i:64 * i + 64, 128 * c:128 * c + 128]


def unpack(received, store):
    for i in range(2):
        for c in range(6):
            store(i, c, received[:, 6 * i + c, :])


def greet(extra):
    t, q = place()
    barrier = pltpu.get_barrier_semaphore()

    for peer in others():
        pl.semaphore_signal(barrier, inc=1, device_id=(peer, q), device_id_type=MESH)

    for peer in extra:
        pl.semaphore_signal(barrier, inc=1, device_id=peer, device_id_type=MESH)


def greeted(extra):
    pl.semaphore_wait(pltpu.get_barrier_semaphore(), 63 + len(extra))


def exchange_start(send, received, sems):
    t, q = place()

    for peer in others():
        pltpu.make_async_remote_copy(
            send.at[peer], received.at[t], sems.at[0], sems.at[1], device_id=(peer, q), device_id_type=MESH
        ).start()

    received[pl.ds(t, 1)] = send[pl.ds(t, 1)]


def exchange_wait(send, received, sems):
    t, q = place()
    all_bytes = pltpu.make_async_remote_copy(
        send.at[pl.ds(0, 63)], received.at[pl.ds(0, 63)], sems.at[0], sems.at[1], device_id=(t ^ 1, q), device_id_type=MESH
    )
    all_bytes.wait_send()
    all_bytes.wait_recv()


def own_rows(w_ref, rows):
    t, _ = place()
    base = pl.multiple_of(t // 2 * 24 + lax.rem(t, 2) * 8, 8)
    wide = w_ref[pl.ds(base, 16), :]
    rows[...] = jnp.where(lax.rem(t, 2) == 0, wide[:12], wide[4:])


def bits():
    t, q = place()
    x, yh, yl, z0 = lax.rem(t, 4), lax.rem(t // 4, 2), q // 2, lax.rem(t // 8, 2)
    return {"a": lax.rem(x, 2) ^ (x // 2), "b": x // 2, "c": yl ^ yh, "d": yh, "e": z0, "f": z0}


def partner(dim):
    t, q = place()
    if dim == "f":
        return (lax.rem(t + jnp.where(lax.rem(t // 8, 2) == 0, 56, 8), 64), q)
    return {"a": (t ^ 1, q), "b": (t ^ 3, q), "c": (t, q ^ 2), "d": (t ^ 4, q ^ 2), "e": (t ^ 8, q)}[dim]


AXIS = {"a": (0, 1), "c": (1, 0), "d": (3, None), "b": (4, None), "e": (2, None), "f": (2, None)}
SUBS = (
    ((None, 0, 128, "eabcd"), (None, 128, 128, "fbcda"), (0, 256, 128, "cdab"), (1, 256, 128, "dabc")),
    ((None, 0, 128, "ecdab"), (None, 128, 128, "fdabc"), (0, 256, 128, "abcd"), (1, 256, 128, "bcda")),
    ((0, 0, 256, "cdab"), (0, 256, 128, "dabc"), (1, 0, 256, "abcd"), (1, 256, 128, "bcda")),
    ((0, 0, 256, "dabc"), (0, 256, 128, "abcd"), (1, 0, 256, "bcda"), (1, 256, 128, "cdab")),
)
BY_Z = (0, 1)
PLAN = (
    'value',
    0,
    'scores',
    1,
    2,
    (0, 0),
    (1, 0),
    'norm',
    (0, 1),
    (2, 0),
    (1, 1),
    (0, 2),
    (3, 0),
    (2, 1),
    (1, 2),
    'return',
    'take',
    (0, 3),
    (3, 1),
    (2, 2),
    (1, 3),
    (0, 4),
    (3, 2),
    (1, 4),
    (2, 3),
    (3, 3),
)


def order(chunk, sub):
    return SUBS[chunk][sub][3]


def extents(chunk, sub, step):
    size = [2, 2, 2 if SUBS[chunk][sub][0] is None else 1, 2, 2]
    for dim in order(chunk, sub)[:step + 1]:
        size[AXIS[dim][0]] = 1
    return size


def select(chunk, sub, step, own, other):
    z0 = SUBS[chunk][sub][0]
    at = [pl.ds(0, 2), pl.ds(0, 2), pl.ds(0, 2) if z0 is None else pl.ds(z0, 1), pl.ds(0, 2), pl.ds(0, 2)]
    for s, dim in enumerate(order(chunk, sub)[:step + 1]):
        axis, place_in = AXIS[dim]
        bit = own[dim] if place_in is None else own[dim] ^ ((chunk >> place_in) & 1)
        at[axis] = pl.ds(1 - bit if other and s == step else bit, 1)
    return at


def reduce_copy(chunk, sub, step, own, terms, landing, sems):
    _, col, cols, dims = SUBS[chunk][sub]
    return pltpu.make_async_remote_copy(
        terms.at[(chunk, *select(chunk, sub, step, own, True), slice(None), pl.ds(col, cols))],
        landing[chunk, sub, step],
        sems.at[0, step, 4 * chunk + sub],
        sems.at[1, step, 4 * chunk + sub],
        device_id=partner(dims[step]),
        device_id_type=MESH,
    )


def reduce_add(chunk, sub, step, own, terms, landing):
    _, col, cols, _ = SUBS[chunk][sub]
    at = select(chunk, sub, step, own, False)
    size = extents(chunk, sub, step)
    buf = landing[chunk, sub, step]
    for n in range(size[0] * size[1] * size[2] * size[3] * size[4]):
        pos, left = [0] * 5, n
        for axis in (4, 3, 2, 1, 0):
            pos[axis], left = left % size[axis], left // size[axis]
        idx = (chunk, *(s.start + o for s, o in zip(at, pos)), slice(None), slice(col, col + cols))
        terms[idx] = terms[idx] + buf[tuple(pos)]


def landings():
    return [(k, s, step) for k in range(4) for s in range(4) for step in range(len(order(k, s)))]


def landing_shapes():
    return [pltpu.VMEM(tuple(extents(*key)) + (24, SUBS[key[0]][key[1]][2]), F32) for key in landings()]


def group_peers():
    t, q = place()
    return [(t ^ dx, q ^ dq) for dx in (1, 0) for dq in (3, 2, 1, 0) if dx or dq]


def sibling_copy(src, dst, sems, k):
    t, q = place()
    return pltpu.make_async_remote_copy(src, dst, sems.at[0, k], sems.at[1, k], device_id=(t, q ^ 1), device_id_type=MESH)


def join_left(ref, j, own, theirs):
    hi, lo = split(rows2(own, theirs).T)
    ref[j, :, :256] = hi
    ref[j, :, 256:512] = lo
    ref[j, :, 512:] = hi


def join_right(ref, j, own, theirs):
    hi, lo = split(rows2(own, theirs))
    ref[j, :256] = hi
    ref[j, 256:512] = hi
    ref[j, 512:] = lo


def layer_kernel(
    tok_hbm, up_hbm, g_ref, wq_hbm, wo_hbm,
    o_hbm, g_hbm, p_hbm, w_hbm,
    tok, wq, wo, wrows, up,
    wqh, wql, woh, wol, t_ref, u_ref, out, tg, xhat, inv, qkv, probs, mix, dmix, dqkv,
    send_t, send_u, send_o, send_g, recv_t, recv_u, recv_o, recv_g,
    s_xhat, s_mix, s_u, s_v, s_k, s_q, left, right, terms, recv_z, own_piece, pieces,
    *rest,
):
    landing = dict(zip(landings(), rest))
    sem_in, sem_t, sem_u, sem_o, sem_g, sem_sib, sem_red, sem_z, sem_p, sem_out = rest[len(landing):]
    t, q = place()
    z, core = t // 8, lax.rem(q, 2)
    own = bits()
    peers = group_peers()
    extra = [(pt, pq) for pt, pq in peers[:3] + peers[4:]] + [(t ^ 4, q ^ 2)]
    loads = [
        pltpu.make_async_copy(src, dst, sem_in.at[k])
        for k, (src, dst) in enumerate(((tok_hbm, tok), (up_hbm, up), (wq_hbm, wq), (wo_hbm, wo)))
    ]
    loads[0].start()
    loads[1].start()
    recv_z[...] = jnp.zeros_like(recv_z)
    greet(extra)
    loads[0].wait()
    pack(tok, send_t)
    greeted(extra)
    exchange_start(send_t, recv_t, sem_t)
    loads[1].wait()
    pack(up, send_u)
    exchange_start(send_u, recv_u, sem_u)
    loads[2].start()
    loads[3].start()
    loads[2].wait()
    prep_weights(wq, wqh, wql, 256)
    own_rows(wq, wrows)
    loads[3].wait()
    prep_weights(wo, woh, wol, 256)
    gain = g_ref[...].reshape(1, 768)

    def into(ref):
        def store(i, c, v):
            ref[64 * i:64 * i + 64, 128 * c:128 * c + 128] = v

        return store

    exchange_wait(send_t, recv_t, sem_t)
    unpack(recv_t, into(t_ref))
    forward(t_ref[...], gain, wqh, wql, woh, wol, xhat, inv, qkv, probs, mix, out)
    sib = [sibling_copy(xhat, s_xhat, sem_sib, 0), sibling_copy(mix, s_mix, sem_sib, 1)]
    for copy in sib:
        copy.start()
    pack(out, send_o)
    exchange_start(send_o, recv_o, sem_o)
    for k, (a, b) in enumerate(((xhat, s_xhat), (mix, s_mix))):
        sib[k].wait()
        join_left(left, k, a[...], b[...])
    exchange_wait(send_u, recv_u, sem_u)
    unpack(recv_u, into(u_ref))

    def half(ref, start, k):
        return ref.at[:, pl.ds(pl.multiple_of(start + k * 384, 128), 384)]

    sources = ((u_ref, 0, s_u), (dqkv, 1536, s_v), (dqkv, 768, s_k), (dqkv, 0, s_q))

    def share(k):
        ref, start, landed = sources[k]
        return sibling_copy(half(ref, start, 1 - core), landed, sem_sib, 2 + k)

    def chunk(*ks):
        for k in ks:
            share(k).wait()
            ref, start, landed = sources[k]
            join_right(right, k, half(ref, start, core)[...], landed[...])
        for r in range(4):
            rows = left[1 if ks[0] == 0 else 0, 192 * r:192 * r + 192, :]
            both = dot(rows, jnp.concatenate([right[k] for k in ks], 1))
            for n, k in enumerate(ks):
                terms[k, r // 2, r % 2] = both[:, 384 * n:384 * n + 384].reshape(2, 2, 2, 24, 384)
        for k in ks:
            for s in range(4):
                reduce_copy(k, s, 0, own, terms, landing, sem_red).start()

    a, c = own["a"], own["c"]

    def arrive(k, step):
        for s in (range(4) if k in BY_Z else (1, 3, 0, 2)):
            steps = len(order(k, s))
            if step >= steps:
                continue
            reduce_copy(k, s, step, own, terms, landing, sem_red).wait_recv()
            reduce_add(k, s, step, own, terms, landing)
            if step < steps - 1:
                reduce_copy(k, s, step + 1, own, terms, landing, sem_red).start()
        if step < max(len(order(k, s)) for s in range(4)) - 1:
            return
        z2, z1 = a ^ (k >> 1), c ^ (k & 1)
        for z0 in range(2):
            to = 4 * z2 + 2 * z1 + z0
            block = terms.at[k, z2, z1, z0, own["d"], own["b"]]
            far = {"device_id": (to * 8 + lax.rem(t, 8), q), "device_id_type": MESH}

            @pl.when((z != to) & (own["e"] == z0))
            def _(block=block, far=far):
                pltpu.make_async_remote_copy(block, recv_z.at[z], sem_z.at[0], sem_z.at[3], **far).start()

            @pl.when(own["e"] != z0)
            def _(block=block, far=far):
                if k in BY_Z:
                    last = pl.ds(256, 128)
                    pltpu.make_async_remote_copy(
                        block.at[:, last], recv_z.at[z, :, last], sem_z.at[1], sem_z.at[4], **far
                    ).start()
                else:
                    pltpu.make_async_remote_copy(block, recv_z.at[z], sem_z.at[2], sem_z.at[4], **far).start()

            @pl.when(z == to)
            def _(block=block):
                recv_z[pl.ds(z, 1)] = block[...].reshape(1, 24, 384)

    results = [
        pltpu.make_async_copy(src, dst, sem_out.at[k])
        for k, (src, dst) in enumerate(((out, o_hbm), (tg, g_hbm), (wrows, w_hbm), (pieces, p_hbm)))
    ]
    share(0).start()
    for task in PLAN:
        if task == "value":
            back_values(u_ref[...], woh, wol, probs, dmix, dqkv)
            share(1).start()
        elif task == "scores":
            back_scores(qkv, probs, dmix, dqkv)
            share(2).start()
            share(3).start()
        elif task == "norm":
            backward_norm(u_ref[...], gain, wqh, wql, xhat, inv, dqkv, tg)
        elif task == "take":
            exchange_wait(send_o, recv_o, sem_o)
            unpack(recv_o, into(out))
            results[0].start()
            results[2].start()
        elif task == "return":
            pack(tg, send_g)
            exchange_start(send_g, recv_g, sem_g)
        elif isinstance(task, int):
            chunk(*((2, 3) if task == 2 else (task,)))
        else:
            arrive(*task)

    exchange_wait(send_g, recv_g, sem_g)
    unpack(recv_g, into(tg))
    results[1].start()
    held = (a ^ (z // 4)) * 2 + (c ^ lax.rem(z // 2, 2))

    def landed(n, cols, k):
        ref = recv_z.at[pl.ds(0, n), :, pl.ds(0, cols)]
        return pltpu.make_async_copy(ref, ref, sem_z.at[k])

    landed(3, 384, 0).wait()
    landed(2, 128, 1).wait()
    landed(2, 384, 2).wait()
    landed(3, 384, 3).wait()

    @pl.when(held < 2)
    def _():
        landed(4, 128, 4).wait()

    @pl.when(held >= 2)
    def _():
        landed(4, 384, 4).wait()

    total = recv_z[0]
    for k in range(1, 8):
        total = total + recv_z[k]
    own_piece[0] = total[:12]
    own_piece[1] = total[12:]
    me = core * 4 + held
    copies = []
    for k, (pt, pq) in enumerate(peers):
        copy = pltpu.make_async_remote_copy(
            own_piece.at[lax.rem(pt, 2)], pieces.at[me], sem_p.at[0, k], sem_p.at[1, k], device_id=(pt, pq), device_id_type=MESH
        )
        copy.start()
        copies.append(copy)
    pieces[pl.ds(me, 1)] = own_piece[pl.ds(lax.rem(t, 2), 1)]
    for copy in copies:
        copy.wait()
    results[3].start()
    for k, s, step in landings():
        reduce_copy(k, s, step, own, terms, landing, sem_red).wait_send()
    for result in results:
        result.wait()


def finish_kernel(
    o_hbm, g_hbm, p_hbm, w_hbm, gain_hbm, out, tg, qkv_out, out_out, gain_out,
    o_ref, g_ref, pieces, wrows, gain_ref, qkv_rows, out_rows, gain_rows, sems,
):
    t, _ = place()
    pairs = ((p_hbm, pieces), (w_hbm, wrows), (gain_hbm, gain_ref), (o_hbm, o_ref), (g_hbm, g_ref))
    loads = [pltpu.make_async_copy(src, dst, sems.at[k]) for k, (src, dst) in enumerate(pairs)]
    pairs = ((qkv_rows, qkv_out), (out_rows, out_out), (gain_rows, gain_out), (o_ref, out), (g_ref, tg))
    stores = [pltpu.make_async_copy(src, dst, sems.at[5 + k]) for k, (src, dst) in enumerate(pairs)]
    for load in loads:
        load.start()
    for load in loads[:3]:
        load.wait()
    lane = lax.broadcasted_iota(jnp.int32, (12, 768), 1)
    row = lax.broadcasted_iota(jnp.int32, (12, 768), 0)
    gain = jnp.sum(jnp.where(lane == row + 12 * t, gain_ref[...].reshape(1, 768), 0.0), axis=1, keepdims=True)
    gain_sum = jnp.zeros((12, 1), F32)
    for k in range(8):
        chunk, c = k % 4, k // 4
        piece = pieces[k]
        if chunk:
            col = 768 * (3 - chunk) + 384 * c
            qkv_rows[:, col:col + 384] = piece * gain
            gain_sum = gain_sum + jnp.sum(piece * wrows[:, col:col + 384], axis=1, keepdims=True)
        else:
            out_rows[:, 384 * c:384 * c + 384] = piece
    gain_rows[...] = gain_sum.reshape(12)
    for store in stores[:3]:
        store.start()
    for load, store in zip(loads[3:], stores[3:]):
        load.wait()
        store.start()
    for store in stores:
        store.wait()


def body(tokens, norm_gain_vector, qkv_weight, out_weight, upstream):
    shape = tokens.shape
    tok, up = tokens.reshape(128, 768), upstream.reshape(128, 768)
    vmem, hbm = pl.BlockSpec(memory_space=pltpu.VMEM), pl.BlockSpec(memory_space=pl.ANY)
    S = lambda *s: jax.ShapeDtypeStruct(s, F32)
    V = lambda *s: pltpu.VMEM(s, F32)
    H = lambda *s: pltpu.VMEM(s, BF16)
    D = lambda *s: pltpu.SemaphoreType.DMA(s)
    rows = V(128, 768)
    pack_buffer = V(64, 12, 128)
    out_in, tg_in, pieces, wrows = pl.pallas_call(
        layer_kernel,
        out_shape=[S(128, 768), S(128, 768), S(8, 12, 384), S(12, 2304)],
        in_specs=[hbm, hbm, vmem, hbm, hbm],
        out_specs=[hbm] * 4,
        scratch_shapes=[rows, V(768, 2304), V(768, 768), V(12, 2304), rows]
        + [H(768, 2304), H(768, 2304), H(768, 768), H(768, 768)]
        + [rows, rows, rows, rows, rows, V(128, 128), V(128, 2304), V(128, 1536), rows, rows, V(128, 2304)]
        + [pack_buffer] * 8
        + [rows, rows, V(128, 384), V(128, 384), V(128, 384), V(128, 384), H(2, 768, 768), H(4, 768, 384)]
        + [V(4, 2, 2, 2, 2, 2, 24, 384), V(8, 24, 384), V(2, 12, 384), V(8, 12, 384)]
        + landing_shapes()
        + [D(4), D(2), D(2), D(2), D(2), D(2, 6), D(2, 5, 16), D(5), D(2, 7), D(4)],
        compiler_params=pltpu.CompilerParams(collective_id=0, has_side_effects=True, vmem_limit_bytes=60 * 2 ** 20),
    )(tok, up, norm_gain_vector, qkv_weight, out_weight)
    out, tg, qkv_rows, out_rows, gain_rows = pl.pallas_call(
        finish_kernel,
        out_shape=[S(128, 768), S(128, 768), S(12, 2304), S(12, 768), S(12)],
        in_specs=[hbm] * 5,
        out_specs=[hbm] * 5,
        scratch_shapes=[rows, rows, V(8, 12, 384), V(12, 2304), V(768), V(12, 2304), V(12, 768), V(12), D(10)],
        compiler_params=pltpu.CompilerParams(vmem_limit_bytes=60 * 2 ** 20),
    )(out_in, tg_in, pieces, wrows, norm_gain_vector)
    return out.reshape(shape), tg.reshape(shape), qkv_rows, out_rows, gain_rows


def solution(mesh):
    whole = P(None, "tm", "patch", None)
    rows = P("tm", None)
    return jax.shard_map(
        body,
        mesh=mesh,
        in_specs=(whole, P(), P(), P(), whole),
        out_specs=(whole, whole, rows, rows, P("tm")),
        check_vma=False,
    )
```
